32 devices in a mesh: delay: 8 (over z, x), src: 2 (over y), tgt: 2 (over core).
Axes of the slice: x: 2, y: 2, z: 4, core: 2. Of those that a mesh axis runs over, the one named last changes fastest.
Arguments:
- blocks: bfloat16 [8, 2, 2, 32, 128, 128], P('delay', 'src', 'tgt'), may hold values from -0.15625 to 0.15625
- coords: int32 [8, 2, 2, 32, 2], P('delay', 'src', 'tgt'), may hold values from 0 to 31, as said below
- counts: int32 [8, 2, 2], P('delay', 'src', 'tgt'), may hold values from 16 to 32, as said below
- history: bfloat16 [8, 2, 4096, 128], P('delay', None, 'src'), may hold values from -6 to 6
- excitation: bfloat16 [2, 2, 4096, 128], P(None, 'tgt', 'src'), may hold values from -6 to 6
- inverse: bfloat16 [2, 32, 128, 128], P('tgt', 'src'), may hold values from -0.5 to 0.5
Outputs:
- currents: bfloat16 [2, 2, 4096, 128], P(None, 'tgt', 'src')
The draws below stay inside these ranges and needn't reach their ends.
Inputs may be any that keep to these rules, and one draw needn't show every extreme that they name: `counts`: at most 32 used slots in a tile; in every draw some tile has exactly 32. `coords`: within one tile the 32 slots name distinct (row block, column block) pairs, row blocks below 32 and column blocks below 32; slots at or past the tile's count are not used.
All inputs are finite; a program needn't handle non-finite values.
Results may differ from the reference program's by a relative error of at most 0.017.
Values may be sent and summed in bfloat16 or wider, within the bound.
No kernel may reach another device: no remote copies, remote signals or barrier semaphores. Data moves between devices by JAX's collectives and lax.ppermute only.
A program may use at most 64 MiB of HBM per device.

```python
import jax
import jax.numpy as jnp
from jax import lax

E = 128
BLK = 128
N = 8192
CAP = 32
STEPS = 2
BINS = 8
N_SRC = 2
N_TGT = 2


def draw_counts(key, part):
    tile_count = BINS * N_SRC * N_TGT
    values = jax.random.randint(key, (tile_count,), CAP // 2, CAP + 1)
    chosen = jax.random.randint(jax.random.fold_in(key, 7), (), 0, tile_count)
    values = values.at[chosen].set(CAP)
    return values.reshape(BINS, N_SRC, N_TGT).astype(jnp.int32)


def draw_coords(key, part):
    row_count = N // (N_TGT * BLK)
    col_count = N // (N_SRC * BLK)
    places = row_count * col_count
    tile_count = BINS * N_SRC * N_TGT
    scores = jax.random.randint(key, (tile_count, places), 0, 1 << 16) * places
    scores = scores + jnp.arange(places, dtype=jnp.int32)[None, :]
    ranked = jnp.argsort(scores, axis=1)[:, :CAP].astype(jnp.int32)
    pairs = jnp.stack([ranked // col_count, ranked % col_count], axis=-1)
    return pairs.reshape(BINS, N_SRC, N_TGT, CAP, 2).astype(jnp.int32)


def block_scale(rng, dims, split, low, largest):
    def one(position, blocks):
        heights = jax.random.uniform(jax.random.fold_in(jax.random.fold_in(rng, 6), position), (blocks,), jnp.float32, low / len(split), largest / len(split))
        return jnp.repeat(jnp.exp(heights), dims[position] // blocks).reshape((-1,) + (1,) * (len(dims) - position - 1))

    factor_of = one(*split[0])
    for cut in split[1:]:
        factor_of = factor_of * one(*cut)
    return factor_of


def normal_values(stream_key, dims, width, most, cuts=(), held_as=jnp.bfloat16):
    array = width * jax.random.normal(stream_key, dims, jnp.float32)
    if cuts:
        array = array * block_scale(stream_key, dims, cuts, -0.22, 0.18)
    return jnp.clip(array, -most, most).astype(held_as)


def setup_inputs(seed: int = 0) -> dict:
    key_list = jax.random.split(jax.random.key(seed), 7)
    return {
        "blocks": normal_values(key_list[0], (BINS, N_SRC, N_TGT, CAP, BLK, BLK), (3 * CAP * N_SRC * BINS * BLK * BLK * N_TGT // (4 * N)) ** -0.5, 0.15625, ((0, 8), (1, 2), (2, 2))),
        "coords": draw_coords(jax.random.fold_in(key_list[6], 71), 0),
        "counts": draw_counts(jax.random.fold_in(key_list[6], 71), 0),
        "history": normal_values(key_list[3], (BINS, N_TGT, N // N_TGT, E), 1.0, 6.0, ((0, 8), (2, 2))),
        "excitation": normal_values(key_list[4], (STEPS, N_TGT, N // N_TGT, E), 1.0, 6.0, ((1, 2), (2, 2))),
        "inverse": normal_values(key_list[5], (N_TGT, N // (N_TGT * BLK), BLK, BLK), BLK ** -0.5, 0.5, ((0, 2), (1, 2))),
    }


def tile_partial(slot_blocks, slot_places, slot_total, tile_cur):
    col_count = N // (N_SRC * BLK)
    row_count = N // (N_TGT * BLK)
    pieces = tile_cur.reshape(col_count, BLK, E)[slot_places[:, 1]]
    live_slots = (lax.iota(jnp.int32, CAP) < slot_total).astype(jnp.float32)
    products = jnp.einsum("cij,cjw->ciw", slot_blocks.astype(jnp.float32), pieces.astype(jnp.float32))
    products = products * live_slots[:, None, None]
    summed = jax.ops.segment_sum(products, slot_places[:, 0], num_segments=row_count)
    return summed.reshape(row_count * BLK, E)


def reference(blocks, coords, counts, history, excitation, inverse):
    owned_rows = N // (N_TGT * N_SRC)
    row_count = N // (N_TGT * BLK)
    results = []
    for moment in range(STEPS):
        if moment > 0:
            earlier = jnp.stack([results[moment - 1 - lag] for lag in range(moment)])
            lagged = jnp.concatenate([earlier, history[: BINS - moment]], axis=0)
        else:
            lagged = history

        def add_bin(bin_index, field_sum):
            tile_set = lagged[bin_index].reshape(N_TGT, N_SRC, owned_rows, E).transpose(1, 0, 2, 3)
            inner = jax.vmap(tile_partial, in_axes=(0, 0, 0, None))
            per_tile = jax.vmap(inner, in_axes=(0, 0, 0, 0))(blocks[bin_index], coords[bin_index], counts[bin_index], tile_set)
            rounded = lax.optimization_barrier(per_tile.astype(jnp.bfloat16)).astype(jnp.float32)
            return field_sum + jnp.sum(rounded, axis=0)

        field_sum = lax.fori_loop(0, BINS, add_bin, jnp.zeros((N_TGT, N // N_TGT, E), jnp.float32))
        drive_rows = (excitation[moment].astype(jnp.float32) - field_sum).astype(jnp.bfloat16)
        drive_rows = drive_rows.reshape(N_TGT, row_count, BLK, E)
        current = jnp.einsum("tbij,tbjw->tbiw", inverse.astype(jnp.float32), drive_rows.astype(jnp.float32))
        results.append(current.reshape(N_TGT, N // N_TGT, E).astype(jnp.bfloat16))
    return jnp.stack(results)
```

```python
import functools

import jax
import jax.numpy as jnp
from jax import lax
from jax.experimental import pallas as pl
from jax.experimental.pallas import tpu as pltpu
from jax.sharding import PartitionSpec as P

VMEM = pl.BlockSpec(memory_space=pltpu.VMEM)
SMEM = pl.BlockSpec(memory_space=pltpu.SMEM)
PARAMS = pltpu.CompilerParams(vmem_limit_bytes=48 * 1024 * 1024)
F32 = jnp.float32
BF16 = jnp.bfloat16


def exchange(array, axis, by):
    peers = lax.axis_size(axis)
    return lax.ppermute(array, axis, [(i, i ^ by) for i in range(peers)])


def call(kernel, outs, specs, scratch, *args):
    return pl.pallas_call(
        kernel,
        out_shape=outs,
        in_specs=specs,
        out_specs=[VMEM] * len(outs),
        scratch_shapes=scratch,
        compiler_params=PARAMS,
    )(*args)


class Plan:
    def __init__(self, blocks, history):
        self.edge = blocks.shape[-1]
        self.slots = blocks.shape[3]
        self.owned = history.shape[2]
        self.width = history.shape[3]
        self.srcs = lax.axis_size("src")
        self.bins = lax.axis_size("delay")
        self.halves = history.shape[1]
        owned_blocks = self.owned // self.edge
        self.groups = min(self.bins // 2, owned_blocks // 2)
        self.slice_rows = self.owned // (2 * self.groups)
        self.piece = self.slice_rows // 2
        self.tile_rows = self.owned * self.srcs
        self.slices = 2 * self.groups

    def x(self):
        return lax.axis_index("delay") & 1

    def g(self):
        return (lax.axis_index("delay") >> 1) & (self.groups - 1)

    def shape(self, *lead):
        return jax.ShapeDtypeStruct((*lead, self.piece, self.width), BF16)


def tile_product(p, acc, blocks, coords, counts, column):
    acc[...] = jnp.zeros_like(acc)

    def slot(c, carry):
        row = pl.multiple_of(coords[2 * c] * p.edge, p.edge)
        acc[pl.ds(row, p.edge)] += jnp.dot(
            blocks[c], column(coords[2 * c + 1]), preferred_element_type=F32
        )
        return carry

    lax.fori_loop(0, counts[0], slot, 0)


def split_first(p, acc, outs):
    src, x = lax.axis_index("src"), p.x()
    a_outs, b_send, b_keep = outs[: p.srcs], outs[p.srcs], outs[p.srcs + 1]
    unit = p.slice_rows

    def rows(s, xx, g, piece):
        start = ((s * 2 + xx) * p.groups + g) * unit + piece * p.piece
        return acc[pl.ds(pl.multiple_of(start, p.piece), p.piece)].astype(BF16)

    for k, ref in enumerate(a_outs):
        for xx in range(2):
            for g in range(p.groups):
                ref[xx, g] = rows(src ^ k, xx, g, 0)
    for s in range(p.srcs):
        for g in range(p.groups):
            b_send[s, g] = rows(s, x ^ 1, g, 1)
            b_keep[s, g] = rows(s, x, g, 1)


def first_kernel(p, blocks, coords, counts, history, *rest):
    *outs, own_half, acc = rest
    per_half = p.owned // p.edge
    own_half[...] = history[lax.axis_index("tgt")]

    def column(c):
        start = pl.multiple_of((c % per_half) * p.edge, p.edge)
        return history[c // per_half, pl.ds(start, p.edge)]

    tile_product(p, acc, blocks, coords, counts, column)
    split_first(p, acc, outs)


def later_kernel(p, blocks, coords, counts, own, other, *rest):
    *outs, acc = rest
    per_half = p.owned // p.edge
    half = lax.axis_index("tgt")

    def column(c):
        start = pl.multiple_of((c % per_half) * p.edge, p.edge)
        at = pl.ds(start, p.edge)
        return jnp.where(c // per_half == half, own[at], other[at])

    tile_product(p, acc, blocks, coords, counts, column)
    split_first(p, acc, outs)


def second_kernel(p, *refs):
    n = p.srcs
    a_keep, a_came = refs[0], refs[1:n]
    b_keep, b_came = refs[n], refs[n + 1]
    a_send, a_stay = refs[n + 2], refs[n + 3]
    b_outs = refs[n + 4 :]
    src, x = lax.axis_index("src"), p.x()

    def a_sum(xx):
        total = a_keep[xx].astype(F32)
        for came in a_came:
            total = total + came[xx].astype(F32)
        return total.astype(BF16)

    a_send[...] = a_sum(x ^ 1)
    a_stay[...] = a_sum(x)
    for k, ref in enumerate(b_outs):
        s = src ^ k
        ref[...] = (b_keep[s].astype(F32) + b_came[s].astype(F32)).astype(BF16)


def third_kernel(p, *refs):
    n = p.srcs
    a_keep, a_came, b_keep = refs[:3]
    b_came = refs[3 : n + 2]
    outs = refs[n + 2 :]
    mine = p.g()
    for k, ref in enumerate(outs):
        g = mine ^ k
        ref[0] = (a_keep[g].astype(F32) + a_came[g].astype(F32)).astype(BF16)
        total = b_keep[g].astype(F32)
        for came in b_came:
            total = total + came[g].astype(F32)
        ref[1] = total.astype(BF16)


def current_kernel(p, step, keep, *refs):
    *came, excitation, inverse, out = refs
    start = (p.x() * p.groups + p.g()) * p.slice_rows
    per_slice = p.slice_rows // p.edge
    field = keep[...].astype(F32)
    for ref in came:
        field = field + ref[...].astype(F32)
    field = field.reshape(p.slice_rows, p.width)
    at = pl.ds(pl.multiple_of(start, p.slice_rows), p.slice_rows)
    drive = (excitation[step, 0, at].astype(F32) - field).astype(BF16)
    first = (p.x() * p.groups + p.g()) * per_slice
    for b in range(per_slice):
        rows = slice(b * p.edge, (b + 1) * p.edge)
        out[rows] = jnp.dot(
            inverse[0, first + b], drive[rows], preferred_element_type=F32
        ).astype(BF16)


def place_of(p, k):
    low = (lax.axis_index("delay") & (p.slices - 1)) ^ k
    at = ((low & 1) * p.groups + (low >> 1)) * p.slice_rows
    return pl.ds(pl.multiple_of(at, p.slice_rows), p.slice_rows)


def join_kernel(p, *refs):
    *slices, shifted, out, lagged = refs
    for k, ref in enumerate(slices):
        out[place_of(p, k)] = ref[...]
    first_bin = lax.axis_index("delay") == 0

    @pl.when(first_bin)
    def _():
        lagged[...] = out[...]

    @pl.when(jnp.logical_not(first_bin))
    def _():
        lagged[...] = shifted[...]


def last_kernel(p, before, *refs):
    *slices, out = refs
    out[: before.shape[0], 0] = before[...]
    for k, ref in enumerate(slices):
        out[before.shape[0], 0, place_of(p, k)] = ref[...]


def field_sum(p, firsts):
    n = p.srcs
    a_keep, a_sends = firsts[0], firsts[1:n]
    b_send, b_keep = firsts[n], firsts[n + 1]
    a_came = [exchange(v, "src", k) for k, v in enumerate(a_sends, 1)]
    b_came = exchange(b_send, "delay", 1)
    one = p.shape(p.groups)
    a_send, a_stay, b_stay, *b_sends = call(
        functools.partial(second_kernel, p),
        [one] * (2 + n),
        [VMEM] * (n + 2),
        [],
        a_keep,
        *a_came,
        b_keep,
        b_came,
    )
    a_came = exchange(a_send, "delay", 1)
    b_came = [exchange(v, "src", k) for k, v in enumerate(b_sends, 1)]
    terms = call(
        functools.partial(third_kernel, p),
        [p.shape(2)] * p.groups,
        [VMEM] * (n + 2),
        [],
        a_stay,
        a_came,
        b_stay,
        *b_came,
    )
    by = 2 * p.groups
    while by < p.bins:
        terms = [
            (v.astype(F32) + exchange(v, "delay", by).astype(F32)).astype(BF16)
            for v in terms
        ]
        by *= 2
    keep, *sends = terms
    return [keep] + [exchange(v, "delay", 2 * k) for k, v in enumerate(sends, 1)]


def shards(blocks, coords, counts, history, excitation, inverse):
    p = Plan(blocks, history)
    steps = excitation.shape[0]
    slot_blocks = blocks.reshape(blocks.shape[3:])
    places = coords.reshape(-1)
    used = counts.reshape(-1)
    first_outs = (
        [p.shape(2, p.groups)] * p.srcs
        + [p.shape(p.srcs, p.groups)] * 2
    )
    half = jax.ShapeDtypeStruct((p.owned, p.width), BF16)
    acc = [pltpu.VMEM((p.tile_rows, p.width), F32)]
    *firsts, lagged = call(
        functools.partial(first_kernel, p),
        first_outs + [half],
        [VMEM, SMEM, SMEM, VMEM],
        acc,
        slot_blocks,
        places,
        used,
        history[0],
    )
    done = []
    for step in range(steps):
        terms = field_sum(p, firsts)
        piece = call(
            functools.partial(current_kernel, p, step),
            [jax.ShapeDtypeStruct((p.slice_rows, p.width), BF16)],
            [VMEM] * (len(terms) + 2),
            [],
            *terms,
            excitation,
            inverse,
        )[0]
        if step + 1 < steps:
            shifted = lax.ppermute(
                lagged, "delay", [(i, i + 1) for i in range(p.bins - 1)]
            )
        slices = [piece] + [exchange(piece, "delay", k) for k in range(1, p.slices)]
        if step + 1 == steps:
            return call(
                functools.partial(last_kernel, p),
                [jax.ShapeDtypeStruct((steps, 1, p.owned, p.width), BF16)],
                [VMEM] * (1 + len(slices)),
                [],
                jnp.stack(done),
                *slices,
            )[0]
        current, lagged = call(
            functools.partial(join_kernel, p),
            [half, half],
            [VMEM] * (len(slices) + 1),
            [],
            *slices,
            shifted,
        )
        done.append(current)
        other = exchange(lagged, "tgt", 1)
        firsts = call(
            functools.partial(later_kernel, p),
            first_outs,
            [VMEM, SMEM, SMEM, VMEM, VMEM],
            acc,
            slot_blocks,
            places,
            used,
            lagged,
            other,
        )


def solution(mesh):
    placed = (
        P("delay", "src", "tgt", None, None, None),
        P("delay", "src", "tgt", None, None),
        P("delay", "src", "tgt"),
        P("delay", None, "src", None),
        P(None, "tgt", "src", None),
        P("tgt", "src", None, None),
    )
    return jax.shard_map(
        shards, mesh=mesh, in_specs=placed, out_specs=P(None, "tgt", "src", None), check_vma=False
    )
```

```python
import functools

import jax
import jax.numpy as jnp
from jax import lax
from jax.experimental import pallas as pl
from jax.experimental.pallas import tpu as pltpu
from jax.sharding import PartitionSpec as P

VMEM = pl.BlockSpec(memory_space=pltpu.VMEM)
HBM = pl.BlockSpec(memory_space=pltpu.HBM)
SMEM = pl.BlockSpec(memory_space=pltpu.SMEM)
MIB = 1024 * 1024
F32 = jnp.float32
BF16 = jnp.bfloat16


def exchange(array, axis, by):
    peers = lax.axis_size(axis)
    return lax.ppermute(array, axis, [(i, i ^ by) for i in range(peers)])


def call(kernel, outs, specs, scratch, *args, grant=32 * MIB):
    return list(pl.pallas_call(
        kernel,
        out_shape=outs,
        in_specs=specs,
        out_specs=[VMEM] * len(outs),
        scratch_shapes=scratch,
        compiler_params=pltpu.CompilerParams(vmem_limit_bytes=grant),
    )(*args))


class Plan:
    def __init__(self, blocks, history):
        self.edge = blocks.shape[-1]
        self.slots = blocks.shape[3]
        self.owned = history.shape[2]
        self.width = history.shape[3]
        self.srcs = lax.axis_size("src")
        self.bins = lax.axis_size("delay")
        self.halves = history.shape[1]
        owned_blocks = self.owned // self.edge
        self.groups = min(self.bins // 2, owned_blocks // 2)
        self.slice_rows = self.owned // (2 * self.groups)
        self.piece = self.slice_rows // 2
        self.tile_rows = self.owned * self.srcs
        self.slices = 2 * self.groups

    def x(self):
        return lax.axis_index("delay") & 1

    def g(self):
        return (lax.axis_index("delay") >> 1) & (self.groups - 1)

    def shape(self, *lead):
        return jax.ShapeDtypeStruct((*lead, self.piece, self.width), BF16)


GROUP = 4


def tile_product(p, acc, blocks, coords, counts, column, ready=None):
    def group(i, carry):
        if ready is not None:
            ready(i)
        slots = [i * GROUP + j for j in range(GROUP)]

        @pl.when(slots[0] < counts[0])
        def _():
            products = [
                jnp.dot(blocks[c], column(coords[1, c]), preferred_element_type=F32)
                for c in slots
            ]
            for c, product in zip(slots, products):
                at = pl.ds(pl.multiple_of(coords[0, c] * p.edge, p.edge), p.edge)
                acc[at] += jnp.where(c < counts[0], product, 0.0)

        return carry

    lax.fori_loop(0, p.slots // GROUP, group, 0)


def split_first(p, acc, outs):
    src, x = lax.axis_index("src"), p.x()
    a_outs, b_send, b_keep = outs[: p.srcs], outs[p.srcs], outs[p.srcs + 1]
    unit = p.slice_rows

    def rows(s, xx, g, piece):
        start = ((s * 2 + xx) * p.groups + g) * unit + piece * p.piece
        return acc[pl.ds(pl.multiple_of(start, p.piece), p.piece)].astype(BF16)

    for k, ref in enumerate(a_outs):
        for xx in range(2):
            for g in range(p.groups):
                ref[xx, g] = rows(src ^ k, xx, g, 0)
    for s in range(p.srcs):
        for g in range(p.groups):
            b_send[s, g] = rows(s, x ^ 1, g, 1)
            b_keep[s, g] = rows(s, x, g, 1)


def first_kernel(p, blocks_hbm, coords, counts, history_hbm, *rest):
    *outs, own_half, acc, blocks, history, block_sem, history_sem = rest
    per_half = p.owned // p.edge
    rows = p.owned // 2
    copies = [
        pltpu.make_async_copy(
            history_hbm.at[h, pl.ds(i * rows, rows)],
            history.at[h, pl.ds(i * rows, rows)],
            history_sem.at[h, i],
        )
        for h in range(p.halves)
        for i in range(2)
    ]

    def block_copy(i):
        at = pl.ds(i * GROUP, GROUP)
        return pltpu.make_async_copy(blocks_hbm.at[at], blocks.at[at], block_sem.at[i])

    for copy in copies:
        copy.start()
    for i in range(p.slots // GROUP):
        block_copy(i).start()
    acc[...] = jnp.zeros_like(acc)
    for copy in copies:
        copy.wait()

    def column(c):
        start = pl.multiple_of((c % per_half) * p.edge, p.edge)
        return history[c // per_half, pl.ds(start, p.edge)]

    tile_product(p, acc, blocks, coords, counts, column, lambda i: block_copy(i).wait())
    own_half[...] = history[lax.axis_index("tgt")]
    split_first(p, acc, outs)


def later_kernel(p, blocks, coords, counts, own, other, *rest):
    *outs, acc = rest
    per_half = p.owned // p.edge
    half = lax.axis_index("tgt")

    def column(c):
        start = pl.multiple_of((c % per_half) * p.edge, p.edge)
        at = pl.ds(start, p.edge)
        return jnp.where(c // per_half == half, own[at], other[at])

    acc[...] = jnp.zeros_like(acc)
    tile_product(p, acc, blocks, coords, counts, column)
    split_first(p, acc, outs)


def second_kernel(p, *refs):
    n = p.srcs
    a_keep, a_came = refs[0], refs[1:n]
    b_keep, b_came = refs[n], refs[n + 1]
    a_send, a_stay = refs[n + 2], refs[n + 3]
    b_outs = refs[n + 4 :]
    src, x = lax.axis_index("src"), p.x()

    def a_sum(xx):
        total = a_keep[xx].astype(F32)
        for came in a_came:
            total = total + came[xx].astype(F32)
        return total.astype(BF16)

    a_send[...] = a_sum(x ^ 1)
    a_stay[...] = a_sum(x)
    for k, ref in enumerate(b_outs):
        s = src ^ k
        ref[...] = (b_keep[s].astype(F32) + b_came[s].astype(F32)).astype(BF16)


def third_kernel(p, *refs):
    n = p.srcs
    a_keep, a_came, b_keep = refs[:3]
    b_came = refs[3 : n + 2]
    outs = refs[n + 2 :]
    if len(outs) > p.groups:
        mine, behind, *outs, onward = outs

        @pl.when(p.x() == 0)
        def _():
            onward[...] = mine[...]

        @pl.when(p.x() == 1)
        def _():
            onward[...] = behind[...]

    mine = p.g()
    for k, ref in enumerate(outs):
        g = mine ^ k
        ref[0] = (a_keep[g].astype(F32) + a_came[g].astype(F32)).astype(BF16)
        total = b_keep[g].astype(F32)
        for came in b_came:
            total = total + came[g].astype(F32)
        ref[1] = total.astype(BF16)


def current_kernel(p, step, keep, *refs):
    *came, excitation, inverse, out = refs
    start = (p.x() * p.groups + p.g()) * p.slice_rows
    per_slice = p.slice_rows // p.edge
    field = keep[...].astype(F32)
    for ref in came:
        field = field + ref[...].astype(F32)
    field = field.reshape(p.slice_rows, p.width)
    at = pl.ds(pl.multiple_of(start, p.slice_rows), p.slice_rows)
    drive = (excitation[step, 0, at].astype(F32) - field).astype(BF16)
    first = (p.x() * p.groups + p.g()) * per_slice
    for b in range(per_slice):
        rows = slice(b * p.edge, (b + 1) * p.edge)
        out[rows] = jnp.dot(
            inverse[0, first + b], drive[rows], preferred_element_type=F32
        ).astype(BF16)


def place_of(p, k):
    low = (lax.axis_index("delay") & (p.slices - 1)) ^ k
    at = ((low & 1) * p.groups + (low >> 1)) * p.slice_rows
    return pl.ds(pl.multiple_of(at, p.slice_rows), p.slice_rows)


def join_kernel(p, *refs):
    *slices, shifted, out, lagged = refs
    for k, ref in enumerate(slices):
        out[place_of(p, k)] = ref[...]
    first_bin = lax.axis_index("delay") == 0

    @pl.when(first_bin)
    def _():
        lagged[...] = out[...]

    @pl.when(jnp.logical_not(first_bin))
    def _():
        lagged[...] = shifted[...]


def last_kernel(p, before, *refs):
    *slices, out = refs
    out[: before.shape[0], 0] = before[...]
    for k, ref in enumerate(slices):
        out[before.shape[0], 0, place_of(p, k)] = ref[...]


def field_sum(p, firsts, lagged):
    n = p.srcs
    moved = []
    if lagged is not None:
        behind = lax.ppermute(
            lagged, "delay", [(i, i + 2) for i in range(1, p.bins - 2, 2)]
        )
        moved = [lagged, behind]
    a_keep, a_sends = firsts[0], firsts[1:n]
    b_send, b_keep = firsts[n], firsts[n + 1]
    a_came = [exchange(v, "src", k) for k, v in enumerate(a_sends, 1)]
    b_came = exchange(b_send, "delay", 1)
    one = p.shape(p.groups)
    a_send, a_stay, b_stay, *b_sends = call(
        functools.partial(second_kernel, p),
        [one] * (2 + n),
        [VMEM] * (n + 2),
        [],
        a_keep,
        *a_came,
        b_keep,
        b_came,
    )
    a_came = exchange(a_send, "delay", 1)
    b_came = [exchange(v, "src", k) for k, v in enumerate(b_sends, 1)]
    terms = call(
        functools.partial(third_kernel, p),
        [p.shape(2)] * p.groups
        + [jax.ShapeDtypeStruct(v.shape, BF16) for v in moved[:1]],
        [VMEM] * (n + 2 + len(moved)),
        [],
        a_stay,
        a_came,
        b_stay,
        *b_came,
        *moved,
    )
    shifted = None
    if moved:
        shifted = exchange(terms.pop(), "delay", 1)
    by = 2 * p.groups
    while by < p.bins:
        terms = [
            (v.astype(F32) + exchange(v, "delay", by).astype(F32)).astype(BF16)
            for v in terms
        ]
        by *= 2
    keep, *sends = terms
    came = [exchange(v, "delay", 2 * k) for k, v in enumerate(sends, 1)]
    return [keep, *came], shifted


def shards(blocks, coords, counts, history, excitation, inverse):
    p = Plan(blocks, history)
    steps = excitation.shape[0]
    slot_blocks = blocks.reshape(blocks.shape[3:])
    places = coords.reshape(-1, 2).T
    used = counts.reshape(-1)
    first_outs = (
        [p.shape(2, p.groups)] * p.srcs
        + [p.shape(p.srcs, p.groups)] * 2
    )
    half = jax.ShapeDtypeStruct((p.owned, p.width), BF16)
    acc = [pltpu.VMEM((p.tile_rows, p.width), F32)]
    *firsts, lagged = call(
        functools.partial(first_kernel, p),
        first_outs + [half],
        [HBM, SMEM, SMEM, HBM],
        acc
        + [
            pltpu.VMEM(slot_blocks.shape, BF16),
            pltpu.VMEM(history.shape[1:], BF16),
            pltpu.SemaphoreType.DMA((p.slots // GROUP,)),
            pltpu.SemaphoreType.DMA((p.halves, 2)),
        ],
        slot_blocks,
        places,
        used,
        history[0],
        grant=52 * MIB,
    )
    done = []
    for step in range(steps):
        more = step + 1 < steps
        terms, shifted = field_sum(p, firsts, lagged if more else None)
        piece = call(
            functools.partial(current_kernel, p, step),
            [jax.ShapeDtypeStruct((p.slice_rows, p.width), BF16)],
            [VMEM] * (len(terms) + 2),
            [],
            *terms,
            excitation,
            inverse,
        )[0]
        slices = [piece] + [exchange(piece, "delay", k) for k in range(1, p.slices)]
        if not more:
            return call(
                functools.partial(last_kernel, p),
                [jax.ShapeDtypeStruct((steps, 1, p.owned, p.width), BF16)],
                [VMEM] * (1 + len(slices)),
                [],
                jnp.stack(done),
                *slices,
            )[0]
        current, lagged = call(
            functools.partial(join_kernel, p),
            [half, half],
            [VMEM] * (len(slices) + 1),
            [],
            *slices,
            shifted,
        )
        done.append(current)
        other = exchange(lagged, "tgt", 1)
        firsts = call(
            functools.partial(later_kernel, p),
            first_outs,
            [VMEM, SMEM, SMEM, VMEM, VMEM],
            acc,
            slot_blocks,
            places,
            used,
            lagged,
            other,
        )


def solution(mesh):
    placed = (
        P("delay", "src", "tgt", None, None, None),
        P("delay", "src", "tgt", None, None),
        P("delay", "src", "tgt"),
        P("delay", None, "src", None),
        P(None, "tgt", "src", None),
        P("tgt", "src", None, None),
    )
    return jax.shard_map(
        shards, mesh=mesh, in_specs=placed, out_specs=P(None, "tgt", "src", None), check_vma=False
    )
```

```python
import functools

import jax
import jax.numpy as jnp
from jax import lax
from jax.experimental import pallas as pl
from jax.experimental.pallas import tpu as pltpu
from jax.sharding import PartitionSpec as P

VMEM = pl.BlockSpec(memory_space=pltpu.VMEM)
HBM = pl.BlockSpec(memory_space=pltpu.HBM)
SMEM = pl.BlockSpec(memory_space=pltpu.SMEM)
MIB = 1024 * 1024
F32 = jnp.float32
BF16 = jnp.bfloat16


def exchange(array, axis, by):
    peers = lax.axis_size(axis)
    return lax.ppermute(array, axis, [(i, i ^ by) for i in range(peers)])


def hop(array, piece, stage):
    bins, srcs, cores = (lax.axis_size(a) for a in ("delay", "src", "tgt"))
    pairs = []
    for d in range(bins):
        for s in range(srcs):
            for t in range(cores):
                over_src = (piece + t + stage) % 2 == 0
                to = (d, s ^ 1) if over_src else (d ^ 1, s)
                pairs.append(
                    ((d * srcs + s) * cores + t, (to[0] * srcs + to[1]) * cores + t)
                )
    return lax.ppermute(array, ("delay", "src", "tgt"), pairs)


def call(kernel, outs, specs, scratch, *args, grant=32 * MIB):
    return list(pl.pallas_call(
        kernel,
        out_shape=outs,
        in_specs=specs,
        out_specs=[VMEM] * len(outs),
        scratch_shapes=scratch,
        compiler_params=pltpu.CompilerParams(vmem_limit_bytes=grant),
    )(*args))


class Plan:
    def __init__(self, blocks, history):
        self.edge = blocks.shape[-1]
        self.slots = blocks.shape[3]
        self.owned = history.shape[2]
        self.width = history.shape[3]
        self.srcs = lax.axis_size("src")
        self.bins = lax.axis_size("delay")
        self.halves = history.shape[1]
        owned_blocks = self.owned // self.edge
        self.groups = min(self.bins // 2, owned_blocks // 2)
        self.slice_rows = self.owned // (2 * self.groups)
        self.piece = self.slice_rows // 2
        self.tile_rows = self.owned * self.srcs
        self.slices = 2 * self.groups

    def x(self):
        return lax.axis_index("delay") & 1

    def g(self):
        return (lax.axis_index("delay") >> 1) & (self.groups - 1)

    def shape(self, *lead):
        return jax.ShapeDtypeStruct((*lead, self.piece, self.width), BF16)


GROUP = 4


def tile_product(p, acc, blocks, coords, counts, column, ready=None):
    def group(i, carry):
        if ready is not None:
            ready(i)
        slots = [i * GROUP + j for j in range(GROUP)]

        @pl.when(slots[0] < counts[0])
        def _():
            products = [
                jnp.dot(blocks[c], column(coords[1, c]), preferred_element_type=F32)
                for c in slots
            ]
            for c, product in zip(slots, products):
                at = pl.ds(pl.multiple_of(coords[0, c] * p.edge, p.edge), p.edge)
                acc[at] += jnp.where(c < counts[0], product, 0.0)

        return carry

    lax.fori_loop(0, p.slots // GROUP, group, 0)


def over_src(piece):
    return ((lax.axis_index("tgt") + piece) & 1) == 0


def split_first(p, source, outs, high):
    y, x = lax.axis_index("src") & 1, p.x()

    def rows(s, xx, g, piece):
        start = (((high * 2 + s) * 2 + xx) * p.groups + g) * p.slice_rows
        start = pl.multiple_of(start + piece * p.piece, p.piece)
        return source[pl.ds(start, p.piece)].astype(BF16)

    for piece in range(2):
        send, keep = outs[2 * piece], outs[2 * piece + 1]
        by_src = over_src(piece)
        for j in range(2):
            for g in range(p.groups):
                send[j, g] = rows(
                    jnp.where(by_src, y ^ 1, j), jnp.where(by_src, j, x ^ 1), g, piece
                )
                keep[j, g] = rows(
                    jnp.where(by_src, y, j), jnp.where(by_src, j, x), g, piece
                )


def split_kernel(p, source, *outs):
    split_first(p, source, outs, 0)


def hand_over(p, acc, outs):
    if p.srcs == 2:
        split_first(p, acc, outs, 0)
    else:
        outs[0][...] = acc[...].astype(BF16)


def first_kernel(p, blocks_hbm, coords, counts, history_hbm, *rest):
    *outs, own_half, acc, blocks, history, block_sem, history_sem = rest
    per_half = p.owned // p.edge
    rows = p.owned // 2
    copies = [
        pltpu.make_async_copy(
            history_hbm.at[h, pl.ds(i * rows, rows)],
            history.at[h, pl.ds(i * rows, rows)],
            history_sem.at[h, i],
        )
        for h in range(p.halves)
        for i in range(2)
    ]

    def block_copy(i):
        at = pl.ds(i * GROUP, GROUP)
        return pltpu.make_async_copy(blocks_hbm.at[at], blocks.at[at], block_sem.at[i])

    for copy in copies:
        copy.start()
    for i in range(p.slots // GROUP):
        block_copy(i).start()
    acc[...] = jnp.zeros_like(acc)
    for copy in copies:
        copy.wait()

    def column(c):
        start = pl.multiple_of((c % per_half) * p.edge, p.edge)
        return history[c // per_half, pl.ds(start, p.edge)]

    tile_product(p, acc, blocks, coords, counts, column, lambda i: block_copy(i).wait())
    own_half[...] = history[lax.axis_index("tgt")]
    hand_over(p, acc, outs)


def later_kernel(p, blocks, coords, counts, own, other, *rest):
    *outs, acc = rest
    per_half = p.owned // p.edge
    half = lax.axis_index("tgt")

    def column(c):
        start = pl.multiple_of((c % per_half) * p.edge, p.edge)
        at = pl.ds(start, p.edge)
        return jnp.where(c // per_half == half, own[at], other[at])

    acc[...] = jnp.zeros_like(acc)
    tile_product(p, acc, blocks, coords, counts, column)
    hand_over(p, acc, outs)


def total(*terms):
    value = terms[0].astype(F32)
    for term in terms[1:]:
        value = value + term.astype(F32)
    return value.astype(BF16)


def second_kernel(p, *refs):
    ins, outs = refs[:4], refs[4:]
    y, x = lax.axis_index("src") & 1, p.x()
    for piece in range(2):
        keep, came = ins[2 * piece : 2 * piece + 2]
        send, stay = outs[2 * piece : 2 * piece + 2]
        own = jnp.where(over_src(piece), x, y)
        send[...] = total(keep[own ^ 1], came[own ^ 1])
        stay[...] = total(keep[own], came[own])


def third_kernel(p, *refs):
    ins, outs = refs[:4], refs[4:]
    if len(outs) > p.groups:
        mine, behind, *outs, onward = outs

        @pl.when(p.x() == 0)
        def _():
            onward[...] = mine[...]

        @pl.when(p.x() == 1)
        def _():
            onward[...] = behind[...]

    here = p.g()
    for k, ref in enumerate(outs):
        g = here ^ k
        for piece in range(2):
            stay, came = ins[2 * piece : 2 * piece + 2]
            ref[piece] = total(stay[g], came[g])


def current_kernel(p, step, keep, *refs):
    *came, excitation, inverse, out = refs
    start = (p.x() * p.groups + p.g()) * p.slice_rows
    per_slice = p.slice_rows // p.edge
    field = keep[...].astype(F32)
    for ref in came:
        field = field + ref[...].astype(F32)
    field = field.reshape(p.slice_rows, p.width)
    at = pl.ds(pl.multiple_of(start, p.slice_rows), p.slice_rows)
    drive = (excitation[step, 0, at].astype(F32) - field).astype(BF16)
    first = (p.x() * p.groups + p.g()) * per_slice
    for b in range(per_slice):
        rows = slice(b * p.edge, (b + 1) * p.edge)
        out[rows] = jnp.dot(
            inverse[0, first + b], drive[rows], preferred_element_type=F32
        ).astype(BF16)


def place_of(p, k):
    low = (lax.axis_index("delay") & (p.slices - 1)) ^ k
    at = ((low & 1) * p.groups + (low >> 1)) * p.slice_rows
    return pl.ds(pl.multiple_of(at, p.slice_rows), p.slice_rows)


def join_slices(p, slices, out):
    k = 0
    for ref in slices:
        for i in range(ref.shape[0] // p.slice_rows):
            by = 2 * (k % p.groups) + k // p.groups
            out[place_of(p, by)] = ref[i * p.slice_rows : (i + 1) * p.slice_rows]
            k += 1


def join_kernel(p, *refs):
    *slices, shifted, out, lagged = refs
    join_slices(p, slices, out)
    first_bin = lax.axis_index("delay") == 0

    @pl.when(first_bin)
    def _():
        lagged[...] = out[...]

    @pl.when(jnp.logical_not(first_bin))
    def _():
        lagged[...] = shifted[...]


def last_kernel(p, before, *refs):
    *slices, out = refs
    out[: before.shape[0], 0] = before[...]
    join_slices(p, slices, out.at[before.shape[0], 0])


def narrow(p, firsts):
    if p.srcs == 2:
        return firsts
    rest = firsts[0]
    by = p.srcs // 2
    while by > 1:
        upper = (lax.axis_index("src") // by) & 1
        size = rest.shape[0] // 2
        keep = lax.dynamic_slice_in_dim(rest, upper * size, size)
        send = lax.dynamic_slice_in_dim(rest, (1 - upper) * size, size)
        rest = total(keep, exchange(send, "src", by))
        by //= 2
    return call(
        functools.partial(split_kernel, p), [p.shape(2, p.groups)] * 4, [VMEM], [], rest
    )


def field_sum(p, firsts, lagged):
    moved = []
    if lagged is not None:
        behind = lax.ppermute(
            lagged, "delay", [(i, i + 2) for i in range(1, p.bins - 2, 2)]
        )
        moved = [lagged, behind]
    send0, keep0, send1, keep1 = narrow(p, firsts)
    one = p.shape(p.groups)
    send0, stay0, send1, stay1 = call(
        functools.partial(second_kernel, p),
        [one] * 4,
        [VMEM] * 4,
        [],
        keep0,
        hop(send0, 0, 0),
        keep1,
        hop(send1, 1, 0),
    )
    terms = call(
        functools.partial(third_kernel, p),
        [p.shape(2)] * p.groups
        + [jax.ShapeDtypeStruct(v.shape, BF16) for v in moved[:1]],
        [VMEM] * (4 + len(moved)),
        [],
        stay0,
        hop(send0, 0, 1),
        stay1,
        hop(send1, 1, 1),
        *moved,
    )
    shifted = None
    if moved:
        shifted = exchange(terms.pop(), "delay", 1)
    by = 2 * p.groups
    while by < p.bins:
        terms = [
            (v.astype(F32) + exchange(v, "delay", by).astype(F32)).astype(BF16)
            for v in terms
        ]
        by *= 2
    keep, *sends = terms
    came = [exchange(v, "delay", 2 * k) for k, v in enumerate(sends, 1)]
    return [keep, *came], shifted


def pack_kernel(*refs):
    *ins, out = refs
    rows = ins[0].shape[0]
    for i, ref in enumerate(ins):
        out[i * rows : (i + 1) * rows] = ref[...]


def pack(p, parts):
    return call(
        pack_kernel,
        [jax.ShapeDtypeStruct((len(parts) * p.slice_rows, p.width), BF16)],
        [VMEM] * len(parts),
        [],
        *parts,
    )[0]


def gather(p, piece):
    along = [exchange(piece, "delay", 2 * k) for k in range(1, p.groups)]
    beside = exchange(piece, "delay", 1)
    return [piece, *along, beside, *(exchange(v, "delay", 1) for v in along)]


def shards(blocks, coords, counts, history, excitation, inverse):
    p = Plan(blocks, history)
    steps = excitation.shape[0]
    slot_blocks = blocks.reshape(blocks.shape[3:])
    places = coords.reshape(-1, 2).T
    used = counts.reshape(-1)
    first_outs = [p.shape(2, p.groups)] * 4
    if p.srcs > 2:
        first_outs = [jax.ShapeDtypeStruct((p.tile_rows, p.width), BF16)]
    half = jax.ShapeDtypeStruct((p.owned, p.width), BF16)
    acc = [pltpu.VMEM((p.tile_rows, p.width), F32)]
    *firsts, lagged = call(
        functools.partial(first_kernel, p),
        first_outs + [half],
        [HBM, SMEM, SMEM, HBM],
        acc
        + [
            pltpu.VMEM(slot_blocks.shape, BF16),
            pltpu.VMEM(history.shape[1:], BF16),
            pltpu.SemaphoreType.DMA((p.slots // GROUP,)),
            pltpu.SemaphoreType.DMA((p.halves, 2)),
        ],
        slot_blocks,
        places,
        used,
        history[0],
        grant=52 * MIB,
    )
    done = []
    for step in range(steps):
        more = step + 1 < steps
        terms, shifted = field_sum(p, firsts, lagged if more else None)
        piece = call(
            functools.partial(current_kernel, p, step),
            [jax.ShapeDtypeStruct((p.slice_rows, p.width), BF16)],
            [VMEM] * (len(terms) + 2),
            [],
            *terms,
            excitation,
            inverse,
        )[0]
        slices = gather(p, piece)
        if not more:
            return call(
                functools.partial(last_kernel, p),
                [jax.ShapeDtypeStruct((steps, 1, p.owned, p.width), BF16)],
                [VMEM] * (1 + len(slices)),
                [],
                jnp.stack(done),
                *slices,
            )[0]
        current, lagged = call(
            functools.partial(join_kernel, p),
            [half, half],
            [VMEM] * (len(slices) + 1),
            [],
            *slices,
            shifted,
        )
        done.append(current)
        other = exchange(lagged, "tgt", 1)
        firsts = call(
            functools.partial(later_kernel, p),
            first_outs,
            [VMEM, SMEM, SMEM, VMEM, VMEM],
            acc,
            slot_blocks,
            places,
            used,
            lagged,
            other,
        )


def solution(mesh):
    placed = (
        P("delay", "src", "tgt", None, None, None),
        P("delay", "src", "tgt", None, None),
        P("delay", "src", "tgt"),
        P("delay", None, "src", None),
        P(None, "tgt", "src", None),
        P("tgt", "src", None, None),
    )
    return jax.shard_map(
        shards, mesh=mesh, in_specs=placed, out_specs=P(None, "tgt", "src", None), check_vma=False
    )
```

```python
import functools

import jax
import jax.numpy as jnp
from jax import lax
from jax.experimental import pallas as pl
from jax.experimental.pallas import tpu as pltpu
from jax.sharding import PartitionSpec as P

VMEM = pl.BlockSpec(memory_space=pltpu.VMEM)
HBM = pl.BlockSpec(memory_space=pltpu.HBM)
SMEM = pl.BlockSpec(memory_space=pltpu.SMEM)
MIB = 1024 * 1024
F32 = jnp.float32
BF16 = jnp.bfloat16


def exchange(array, axis, by):
    peers = lax.axis_size(axis)
    return lax.ppermute(array, axis, [(i, i ^ by) for i in range(peers)])


def hop(array, piece, stage):
    bins, srcs, cores = (lax.axis_size(a) for a in ("delay", "src", "tgt"))
    pairs = []
    for d in range(bins):
        for s in range(srcs):
            for t in range(cores):
                over_src = (piece + t + stage) % 2 == 0
                to = (d, s ^ 1) if over_src else (d ^ 1, s)
                pairs.append(
                    ((d * srcs + s) * cores + t, (to[0] * srcs + to[1]) * cores + t)
                )
    return lax.ppermute(array, ("delay", "src", "tgt"), pairs)


def call(kernel, outs, specs, scratch, *args, grant=32 * MIB):
    return list(pl.pallas_call(
        kernel,
        out_shape=outs,
        in_specs=specs,
        out_specs=[VMEM] * len(outs),
        scratch_shapes=scratch,
        compiler_params=pltpu.CompilerParams(vmem_limit_bytes=grant),
    )(*args))


class Plan:
    def __init__(self, blocks, history):
        self.edge = blocks.shape[-1]
        self.slots = blocks.shape[3]
        self.owned = history.shape[2]
        self.width = history.shape[3]
        self.srcs = lax.axis_size("src")
        self.bins = lax.axis_size("delay")
        self.halves = history.shape[1]
        owned_blocks = self.owned // self.edge
        self.groups = min(self.bins // 2, owned_blocks // 2)
        self.slice_rows = self.owned // (2 * self.groups)
        self.piece = self.slice_rows // 2
        self.tile_rows = self.owned * self.srcs
        self.slices = 2 * self.groups

    def x(self):
        return lax.axis_index("delay") & 1

    def g(self):
        return (lax.axis_index("delay") >> 1) & (self.groups - 1)

    def shape(self, *lead):
        return jax.ShapeDtypeStruct((*lead, self.piece, self.width), BF16)


GROUP = 16


def tile_product(p, acc, blocks, coords, counts, column, ready=None):
    def group(i, carry):
        if ready is not None:
            ready(i)
        slots = [i * GROUP + j for j in range(GROUP)]
        products = [
            jnp.dot(blocks[c], column(coords[1, c]), preferred_element_type=F32)
            for c in slots
        ]
        for c, product in zip(slots, products):
            at = pl.ds(pl.multiple_of(coords[0, c] * p.edge, p.edge), p.edge)
            acc[at] += jnp.where(c < counts[0], product, 0.0)
        return carry

    lax.fori_loop(0, p.slots // GROUP, group, 0, unroll=ready is None)


def over_src(piece):
    return ((lax.axis_index("tgt") + piece) & 1) == 0


def split_first(p, source, outs, high):
    y, x = lax.axis_index("src") & 1, p.x()

    def rows(s, xx, g, piece):
        start = (((high * 2 + s) * 2 + xx) * p.groups + g) * p.slice_rows
        start = pl.multiple_of(start + piece * p.piece, p.piece)
        return source[pl.ds(start, p.piece)].astype(BF16)

    for piece in range(2):
        send, keep = outs[2 * piece], outs[2 * piece + 1]
        by_src = over_src(piece)
        for j in range(2):
            for g in range(p.groups):
                send[j, g] = rows(
                    jnp.where(by_src, y ^ 1, j), jnp.where(by_src, j, x ^ 1), g, piece
                )
                keep[j, g] = rows(
                    jnp.where(by_src, y, j), jnp.where(by_src, j, x), g, piece
                )


def split_kernel(p, source, *outs):
    split_first(p, source, outs, 0)


def hand_over(p, acc, outs):
    if p.srcs == 2:
        split_first(p, acc, outs, 0)
    else:
        outs[0][...] = acc[...].astype(BF16)


def first_kernel(p, blocks_hbm, coords_hbm, counts, history_hbm, *rest):
    *outs, own_half, acc, blocks, history, coords, block_sem, history_sem, coords_sem = rest
    per_half = p.owned // p.edge
    rows = p.owned // 2
    copies = [
        pltpu.make_async_copy(
            history_hbm.at[h, pl.ds(i * rows, rows)],
            history.at[h, pl.ds(i * rows, rows)],
            history_sem.at[h, i],
        )
        for h in range(p.halves)
        for i in range(2)
    ]

    def block_copy(i):
        at = pl.ds(i * GROUP, GROUP)
        return pltpu.make_async_copy(blocks_hbm.at[at], blocks.at[at], block_sem.at[i])

    copies.append(pltpu.make_async_copy(coords_hbm, coords, coords_sem))
    for copy in copies:
        copy.start()
    for i in range(p.slots // GROUP):
        block_copy(i).start()
    acc[...] = jnp.zeros_like(acc)
    for copy in copies:
        copy.wait()

    def column(c):
        start = pl.multiple_of((c % per_half) * p.edge, p.edge)
        return history[c // per_half, pl.ds(start, p.edge)]

    tile_product(p, acc, blocks, coords, counts, column, lambda i: block_copy(i).wait())
    own_half[...] = history[lax.axis_index("tgt")]
    hand_over(p, acc, outs)


def later_kernel(p, blocks, coords, counts, own, other, *rest):
    *outs, acc = rest
    per_half = p.owned // p.edge
    half = lax.axis_index("tgt")

    def column(c):
        start = pl.multiple_of((c % per_half) * p.edge, p.edge)
        at = pl.ds(start, p.edge)
        return jnp.where(c // per_half == half, own[at], other[at])

    acc[...] = jnp.zeros_like(acc)
    tile_product(p, acc, blocks, coords, counts, column)
    hand_over(p, acc, outs)


def total(*terms):
    value = terms[0].astype(F32)
    for term in terms[1:]:
        value = value + term.astype(F32)
    return value.astype(BF16)


def second_kernel(p, *refs):
    ins, outs = refs[:4], refs[4:]
    y, x = lax.axis_index("src") & 1, p.x()
    for piece in range(2):
        keep, came = ins[2 * piece : 2 * piece + 2]
        send, stay = outs[2 * piece : 2 * piece + 2]
        own = jnp.where(over_src(piece), x, y)
        send[...] = total(keep[own ^ 1], came[own ^ 1])
        stay[...] = total(keep[own], came[own])


def third_kernel(p, *refs):
    ins, outs = refs[:4], refs[4:]
    if len(outs) > p.groups:
        mine, behind, *outs, onward = outs

        @pl.when(p.x() == 0)
        def _():
            onward[...] = mine[...]

        @pl.when(p.x() == 1)
        def _():
            onward[...] = behind[...]

    here = p.g()
    for k, ref in enumerate(outs):
        g = here ^ k
        for piece in range(2):
            stay, came = ins[2 * piece : 2 * piece + 2]
            ref[piece] = total(stay[g], came[g])


def current_kernel(p, step, keep, *refs):
    *came, excitation, inverse, out = refs
    start = (p.x() * p.groups + p.g()) * p.slice_rows
    per_slice = p.slice_rows // p.edge
    field = keep[...].astype(F32)
    for ref in came:
        field = field + ref[...].astype(F32)
    field = field.reshape(p.slice_rows, p.width)
    at = pl.ds(pl.multiple_of(start, p.slice_rows), p.slice_rows)
    drive = (excitation[step, 0, at].astype(F32) - field).astype(BF16)
    first = (p.x() * p.groups + p.g()) * per_slice
    for b in range(per_slice):
        rows = slice(b * p.edge, (b + 1) * p.edge)
        out[rows] = jnp.dot(
            inverse[0, first + b], drive[rows], preferred_element_type=F32
        ).astype(BF16)


def place_of(p, k):
    low = (lax.axis_index("delay") & (p.slices - 1)) ^ k
    at = ((low & 1) * p.groups + (low >> 1)) * p.slice_rows
    return pl.ds(pl.multiple_of(at, p.slice_rows), p.slice_rows)


def join_slices(p, slices, out):
    k = 0
    for ref in slices:
        for i in range(ref.shape[0] // p.slice_rows):
            by = 2 * (k % p.groups) + k // p.groups
            out[place_of(p, by)] = ref[i * p.slice_rows : (i + 1) * p.slice_rows]
            k += 1


def join_kernel(p, *refs):
    *slices, shifted, out, lagged = refs
    join_slices(p, slices, out)
    first_bin = lax.axis_index("delay") == 0

    @pl.when(first_bin)
    def _():
        lagged[...] = out[...]

    @pl.when(jnp.logical_not(first_bin))
    def _():
        lagged[...] = shifted[...]


def last_kernel(p, before, *refs):
    *slices, out = refs
    out[: before.shape[0], 0] = before[...]
    join_slices(p, slices, out.at[before.shape[0], 0])


def narrow(p, firsts):
    if p.srcs == 2:
        return firsts
    rest = firsts[0]
    by = p.srcs // 2
    while by > 1:
        upper = (lax.axis_index("src") // by) & 1
        size = rest.shape[0] // 2
        keep = lax.dynamic_slice_in_dim(rest, upper * size, size)
        send = lax.dynamic_slice_in_dim(rest, (1 - upper) * size, size)
        rest = total(keep, exchange(send, "src", by))
        by //= 2
    return call(
        functools.partial(split_kernel, p), [p.shape(2, p.groups)] * 4, [VMEM], [], rest
    )


def field_sum(p, firsts, lagged):
    moved = []
    if lagged is not None:
        behind = lax.ppermute(
            lagged, "delay", [(i, i + 2) for i in range(1, p.bins - 2, 2)]
        )
        moved = [lagged, behind]
    send0, keep0, send1, keep1 = narrow(p, firsts)
    one = p.shape(p.groups)
    send0, stay0, send1, stay1 = call(
        functools.partial(second_kernel, p),
        [one] * 4,
        [VMEM] * 4,
        [],
        keep0,
        hop(send0, 0, 0),
        keep1,
        hop(send1, 1, 0),
    )
    terms = call(
        functools.partial(third_kernel, p),
        [p.shape(2)] * p.groups
        + [jax.ShapeDtypeStruct(v.shape, BF16) for v in moved[:1]],
        [VMEM] * (4 + len(moved)),
        [],
        stay0,
        hop(send0, 0, 1),
        stay1,
        hop(send1, 1, 1),
        *moved,
    )
    shifted = None
    if moved:
        shifted = exchange(terms.pop(), "delay", 1)
    by = 2 * p.groups
    while by < p.bins:
        terms = [
            (v.astype(F32) + exchange(v, "delay", by).astype(F32)).astype(BF16)
            for v in terms
        ]
        by *= 2
    keep, *sends = terms
    came = [exchange(v, "delay", 2 * k) for k, v in enumerate(sends, 1)]
    return [keep, *came], shifted


def pack_kernel(*refs):
    *ins, out = refs
    rows = ins[0].shape[0]
    for i, ref in enumerate(ins):
        out[i * rows : (i + 1) * rows] = ref[...]


def pack(p, parts):
    return call(
        pack_kernel,
        [jax.ShapeDtypeStruct((len(parts) * p.slice_rows, p.width), BF16)],
        [VMEM] * len(parts),
        [],
        *parts,
    )[0]


def gather(p, piece):
    along = [exchange(piece, "delay", 2 * k) for k in range(1, p.groups)]
    beside = exchange(piece, "delay", 1)
    over = [exchange(piece, "delay", 2 * k + 1) if k in (1,) else exchange(v, "delay", 1) for k, v in enumerate(along, 1)]
    return [piece, *along, beside, *over]


def shards(blocks, coords, counts, history, excitation, inverse):
    p = Plan(blocks, history)
    steps = excitation.shape[0]
    slot_blocks = blocks.reshape(blocks.shape[3:])
    places = coords.reshape(-1, 2).T
    used = counts.reshape(-1)
    first_outs = [p.shape(2, p.groups)] * 4
    if p.srcs > 2:
        first_outs = [jax.ShapeDtypeStruct((p.tile_rows, p.width), BF16)]
    half = jax.ShapeDtypeStruct((p.owned, p.width), BF16)
    acc = [pltpu.VMEM((p.tile_rows, p.width), F32)]
    *firsts, lagged = call(
        functools.partial(first_kernel, p),
        first_outs + [half],
        [HBM, HBM, SMEM, HBM],
        acc
        + [
            pltpu.VMEM(slot_blocks.shape, BF16),
            pltpu.VMEM(history.shape[1:], BF16),
            pltpu.SMEM(places.shape, places.dtype),
            pltpu.SemaphoreType.DMA((p.slots // GROUP,)),
            pltpu.SemaphoreType.DMA((p.halves, 2)),
            pltpu.SemaphoreType.DMA,
        ],
        slot_blocks,
        places,
        used,
        history[0],
        grant=52 * MIB,
    )
    done = []
    for step in range(steps):
        more = step + 1 < steps
        terms, shifted = field_sum(p, firsts, lagged if more else None)
        piece = call(
            functools.partial(current_kernel, p, step),
            [jax.ShapeDtypeStruct((p.slice_rows, p.width), BF16)],
            [VMEM] * (len(terms) + 2),
            [],
            *terms,
            excitation,
            inverse,
        )[0]
        slices = gather(p, piece)
        if not more:
            return call(
                functools.partial(last_kernel, p),
                [jax.ShapeDtypeStruct((steps, 1, p.owned, p.width), BF16)],
                [VMEM] * (1 + len(slices)),
                [],
                jnp.stack(done),
                *slices,
            )[0]
        current, lagged = call(
            functools.partial(join_kernel, p),
            [half, half],
            [VMEM] * (len(slices) + 1),
            [],
            *slices,
            shifted,
        )
        done.append(current)
        other = exchange(lagged, "tgt", 1)
        firsts = call(
            functools.partial(later_kernel, p),
            first_outs,
            [VMEM, SMEM, SMEM, VMEM, VMEM],
            acc,
            slot_blocks,
            places,
            used,
            lagged,
            other,
        )


def solution(mesh):
    placed = (
        P("delay", "src", "tgt", None, None, None),
        P("delay", "src", "tgt", None, None),
        P("delay", "src", "tgt"),
        P("delay", None, "src", None),
        P(None, "tgt", "src", None),
        P("tgt", "src", None, None),
    )
    return jax.shard_map(
        shards, mesh=mesh, in_specs=placed, out_specs=P(None, "tgt", "src", None), check_vma=False
    )
```

```python
import functools

import jax
import jax.numpy as jnp
from jax import lax
from jax.experimental import pallas as pl
from jax.experimental.pallas import tpu as pltpu
from jax.sharding import PartitionSpec as P

VMEM = pl.BlockSpec(memory_space=pltpu.VMEM)
HBM = pl.BlockSpec(memory_space=pltpu.HBM)
SMEM = pl.BlockSpec(memory_space=pltpu.SMEM)
MIB = 1024 * 1024
F32 = jnp.float32
BF16 = jnp.bfloat16


def exchange(array, axis, by):
    peers = lax.axis_size(axis)
    return lax.ppermute(array, axis, [(i, i ^ by) for i in range(peers)])


def hop(array, piece, stage):
    bins, srcs, cores = (lax.axis_size(a) for a in ("delay", "src", "tgt"))
    pairs = []
    for d in range(bins):
        for s in range(srcs):
            for t in range(cores):
                over_src = (piece + t + stage) % 2 == 0
                to = (d, s ^ 1) if over_src else (d ^ 1, s)
                pairs.append(
                    ((d * srcs + s) * cores + t, (to[0] * srcs + to[1]) * cores + t)
                )
    return lax.ppermute(array, ("delay", "src", "tgt"), pairs)


def call(kernel, outs, specs, scratch, *args, grant=32 * MIB):
    return list(pl.pallas_call(
        kernel,
        out_shape=outs,
        in_specs=specs,
        out_specs=[VMEM] * len(outs),
        scratch_shapes=scratch,
        compiler_params=pltpu.CompilerParams(vmem_limit_bytes=grant),
    )(*args))


class Plan:
    def __init__(self, blocks, history):
        self.edge = blocks.shape[-1]
        self.slots = blocks.shape[3]
        self.owned = history.shape[2]
        self.width = history.shape[3]
        self.srcs = lax.axis_size("src")
        self.bins = lax.axis_size("delay")
        self.halves = history.shape[1]
        owned_blocks = self.owned // self.edge
        self.groups = min(self.bins // 2, owned_blocks // 2)
        self.slice_rows = self.owned // (2 * self.groups)
        self.piece = self.slice_rows // 2
        self.tile_rows = self.owned * self.srcs
        self.slices = 2 * self.groups

    def x(self):
        return lax.axis_index("delay") & 1

    def g(self):
        return (lax.axis_index("delay") >> 1) & (self.groups - 1)

    def shape(self, *lead):
        return jax.ShapeDtypeStruct((*lead, self.piece, self.width), BF16)


GROUP = 16


def tile_product(p, acc, blocks, coords, counts, column, ready=None):
    def group(i, carry):
        if ready is not None:
            ready(i)
        slots = [i * GROUP + j for j in range(GROUP)]
        products = [
            jnp.dot(blocks[c], column(coords[1, c]), preferred_element_type=F32)
            for c in slots
        ]
        for c, product in zip(slots, products):
            at = pl.ds(pl.multiple_of(coords[0, c] * p.edge, p.edge), p.edge)
            acc[at] += jnp.where(c < counts[0], product, 0.0)
        return carry

    lax.fori_loop(0, p.slots // GROUP, group, 0, unroll=ready is None)


def over_src(piece):
    return ((lax.axis_index("tgt") + piece) & 1) == 0


def split_first(p, source, outs, high):
    y, x = lax.axis_index("src") & 1, p.x()

    def rows(s, xx, g, piece):
        start = (((high * 2 + s) * 2 + xx) * p.groups + g) * p.slice_rows
        start = pl.multiple_of(start + piece * p.piece, p.piece)
        return source[pl.ds(start, p.piece)].astype(BF16)

    for piece in range(2):
        send, keep = outs[2 * piece], outs[2 * piece + 1]
        by_src = over_src(piece)
        for j in range(2):
            for g in range(p.groups):
                send[j, g] = rows(
                    jnp.where(by_src, y ^ 1, j), jnp.where(by_src, j, x ^ 1), g, piece
                )
                keep[j, g] = rows(
                    jnp.where(by_src, y, j), jnp.where(by_src, j, x), g, piece
                )


def split_kernel(p, source, *outs):
    split_first(p, source, outs, 0)


def hand_over(p, acc, outs):
    if p.srcs == 2:
        split_first(p, acc, outs, 0)
    else:
        outs[0][...] = acc[...].astype(BF16)


def first_kernel(p, blocks_hbm, coords_hbm, counts, history_hbm, *rest):
    *outs, own_half, acc, blocks, history, coords, block_sem, history_sem, coords_sem = rest
    per_half = p.owned // p.edge
    rows = p.owned // 2
    copies = [
        pltpu.make_async_copy(
            history_hbm.at[h, pl.ds(i * rows, rows)],
            history.at[h, pl.ds(i * rows, rows)],
            history_sem.at[h, i],
        )
        for h in range(p.halves)
        for i in range(2)
    ]

    def block_copy(i):
        at = pl.ds(i * GROUP, GROUP)
        return pltpu.make_async_copy(blocks_hbm.at[at], blocks.at[at], block_sem.at[i])

    copies.append(pltpu.make_async_copy(coords_hbm, coords, coords_sem))
    for copy in copies:
        copy.start()
    for i in range(p.slots // GROUP):
        block_copy(i).start()
    acc[...] = jnp.zeros_like(acc)
    for copy in copies:
        copy.wait()

    def column(c):
        start = pl.multiple_of((c % per_half) * p.edge, p.edge)
        return history[c // per_half, pl.ds(start, p.edge)]

    tile_product(p, acc, blocks, coords, counts, column, lambda i: block_copy(i).wait())
    own_half[...] = history[lax.axis_index("tgt")]
    hand_over(p, acc, outs)


def later_kernel(p, blocks, coords, counts, own, other, *rest):
    *outs, acc = rest
    per_half = p.owned // p.edge
    half = lax.axis_index("tgt")

    def column(c):
        start = pl.multiple_of((c % per_half) * p.edge, p.edge)
        at = pl.ds(start, p.edge)
        return jnp.where(c // per_half == half, own[at], other[at])

    acc[...] = jnp.zeros_like(acc)
    tile_product(p, acc, blocks, coords, counts, column)
    hand_over(p, acc, outs)


def total(*terms):
    value = terms[0].astype(F32)
    for term in terms[1:]:
        value = value + term.astype(F32)
    return value.astype(BF16)


def second_kernel(p, piece, keep, came, send, stay):
    own = jnp.where(over_src(piece), p.x(), lax.axis_index("src") & 1)
    send[...] = total(keep[own ^ 1], came[own ^ 1])
    stay[...] = total(keep[own], came[own])


def third_kernel(p, *refs):
    ins, outs = refs[:4], refs[4:]
    if len(outs) > p.groups:
        mine, behind, *outs, onward = outs

        @pl.when(p.x() == 0)
        def _():
            onward[...] = mine[...]

        @pl.when(p.x() == 1)
        def _():
            onward[...] = behind[...]

    here = p.g()
    for k, ref in enumerate(outs):
        g = here ^ k
        for piece in range(2):
            stay, came = ins[2 * piece : 2 * piece + 2]
            ref[piece] = total(stay[g], came[g])


def current_kernel(p, step, keep, *refs):
    *came, excitation, inverse, out = refs
    start = (p.x() * p.groups + p.g()) * p.slice_rows
    per_slice = p.slice_rows // p.edge
    field = keep[...].astype(F32)
    for ref in came:
        field = field + ref[...].astype(F32)
    field = field.reshape(p.slice_rows, p.width)
    at = pl.ds(pl.multiple_of(start, p.slice_rows), p.slice_rows)
    drive = (excitation[step, 0, at].astype(F32) - field).astype(BF16)
    first = (p.x() * p.groups + p.g()) * per_slice
    for b in range(per_slice):
        rows = slice(b * p.edge, (b + 1) * p.edge)
        out[rows] = jnp.dot(
            inverse[0, first + b], drive[rows], preferred_element_type=F32
        ).astype(BF16)


def place_of(p, k):
    low = (lax.axis_index("delay") & (p.slices - 1)) ^ k
    at = ((low & 1) * p.groups + (low >> 1)) * p.slice_rows
    return pl.ds(pl.multiple_of(at, p.slice_rows), p.slice_rows)


def join_slices(p, slices, out):
    k = 0
    for ref in slices:
        for i in range(ref.shape[0] // p.slice_rows):
            by = 2 * (k % p.groups) + k // p.groups
            out[place_of(p, by)] = ref[i * p.slice_rows : (i + 1) * p.slice_rows]
            k += 1


def join_kernel(p, *refs):
    *slices, shifted, out, lagged = refs
    join_slices(p, slices, out)
    first_bin = lax.axis_index("delay") == 0

    @pl.when(first_bin)
    def _():
        lagged[...] = out[...]

    @pl.when(jnp.logical_not(first_bin))
    def _():
        lagged[...] = shifted[...]


def last_kernel(p, before, *refs):
    *slices, out = refs
    out[: before.shape[0], 0] = before[...]
    join_slices(p, slices, out.at[before.shape[0], 0])


def narrow(p, firsts):
    if p.srcs == 2:
        return firsts
    rest = firsts[0]
    by = p.srcs // 2
    while by > 1:
        upper = (lax.axis_index("src") // by) & 1
        size = rest.shape[0] // 2
        keep = lax.dynamic_slice_in_dim(rest, upper * size, size)
        send = lax.dynamic_slice_in_dim(rest, (1 - upper) * size, size)
        rest = total(keep, exchange(send, "src", by))
        by //= 2
    return call(
        functools.partial(split_kernel, p), [p.shape(2, p.groups)] * 4, [VMEM], [], rest
    )


def field_sum(p, firsts, lagged):
    moved = []
    if lagged is not None:
        behind = lax.ppermute(
            lagged, "delay", [(i, i + 2) for i in range(1, p.bins - 2, 2)]
        )
        moved = [lagged, behind]
    send0, keep0, send1, keep1 = narrow(p, firsts)
    one = p.shape(p.groups)
    came0, came1 = hop(send0, 0, 0), hop(send1, 1, 0)
    send0, stay0 = call(
        functools.partial(second_kernel, p, 0), [one] * 2, [VMEM] * 2, [], keep0, came0
    )
    send1, stay1 = call(
        functools.partial(second_kernel, p, 1), [one] * 2, [VMEM] * 2, [], keep1, came1
    )
    terms = call(
        functools.partial(third_kernel, p),
        [p.shape(2)] * p.groups
        + [jax.ShapeDtypeStruct(v.shape, BF16) for v in moved[:1]],
        [VMEM] * (4 + len(moved)),
        [],
        stay0,
        hop(send0, 0, 1),
        stay1,
        hop(send1, 1, 1),
        *moved,
    )
    shifted = None
    if moved:
        shifted = exchange(terms.pop(), "delay", 1)
    by = 2 * p.groups
    while by < p.bins:
        terms = [
            (v.astype(F32) + exchange(v, "delay", by).astype(F32)).astype(BF16)
            for v in terms
        ]
        by *= 2
    keep, *sends = terms
    came = [exchange(v, "delay", 2 * k) for k, v in enumerate(sends, 1)]
    return [keep, *came], shifted


def pack_kernel(*refs):
    *ins, out = refs
    rows = ins[0].shape[0]
    for i, ref in enumerate(ins):
        out[i * rows : (i + 1) * rows] = ref[...]


def pack(p, parts):
    return call(
        pack_kernel,
        [jax.ShapeDtypeStruct((len(parts) * p.slice_rows, p.width), BF16)],
        [VMEM] * len(parts),
        [],
        *parts,
    )[0]


def gather(p, piece):
    along = [exchange(piece, "delay", 2 * k) for k in range(1, p.groups)]
    beside = exchange(piece, "delay", 1)
    over = [exchange(piece, "delay", 2 * k + 1) if k in (1,) else exchange(v, "delay", 1) for k, v in enumerate(along, 1)]
    return [piece, *along, beside, *over]


def shards(blocks, coords, counts, history, excitation, inverse):
    p = Plan(blocks, history)
    steps = excitation.shape[0]
    slot_blocks = blocks.reshape(blocks.shape[3:])
    places = coords.reshape(-1, 2).T
    used = counts.reshape(-1)
    first_outs = [p.shape(2, p.groups)] * 4
    if p.srcs > 2:
        first_outs = [jax.ShapeDtypeStruct((p.tile_rows, p.width), BF16)]
    half = jax.ShapeDtypeStruct((p.owned, p.width), BF16)
    acc = [pltpu.VMEM((p.tile_rows, p.width), F32)]
    *firsts, lagged = call(
        functools.partial(first_kernel, p),
        first_outs + [half],
        [HBM, HBM, SMEM, HBM],
        acc
        + [
            pltpu.VMEM(slot_blocks.shape, BF16),
            pltpu.VMEM(history.shape[1:], BF16),
            pltpu.SMEM(places.shape, places.dtype),
            pltpu.SemaphoreType.DMA((p.slots // GROUP,)),
            pltpu.SemaphoreType.DMA((p.halves, 2)),
            pltpu.SemaphoreType.DMA,
        ],
        slot_blocks,
        places,
        used,
        history[0],
        grant=52 * MIB,
    )
    done = []
    for step in range(steps):
        more = step + 1 < steps
        terms, shifted = field_sum(p, firsts, lagged if more else None)
        piece = call(
            functools.partial(current_kernel, p, step),
            [jax.ShapeDtypeStruct((p.slice_rows, p.width), BF16)],
            [VMEM] * (len(terms) + 2),
            [],
            *terms,
            excitation,
            inverse,
        )[0]
        slices = gather(p, piece)
        if not more:
            return call(
                functools.partial(last_kernel, p),
                [jax.ShapeDtypeStruct((steps, 1, p.owned, p.width), BF16)],
                [VMEM] * (1 + len(slices)),
                [],
                jnp.stack(done),
                *slices,
            )[0]
        current, lagged = call(
            functools.partial(join_kernel, p),
            [half, half],
            [VMEM] * (len(slices) + 1),
            [],
            *slices,
            shifted,
        )
        done.append(current)
        other = exchange(lagged, "tgt", 1)
        firsts = call(
            functools.partial(later_kernel, p),
            first_outs,
            [VMEM, SMEM, SMEM, VMEM, VMEM],
            acc,
            slot_blocks,
            places,
            used,
            lagged,
            other,
        )


def solution(mesh):
    placed = (
        P("delay", "src", "tgt", None, None, None),
        P("delay", "src", "tgt", None, None),
        P("delay", "src", "tgt"),
        P("delay", None, "src", None),
        P(None, "tgt", "src", None),
        P("tgt", "src", None, None),
    )
    return jax.shard_map(
        shards, mesh=mesh, in_specs=placed, out_specs=P(None, "tgt", "src", None), check_vma=False
    )
```

```python
import functools

import jax
import jax.numpy as jnp
from jax import lax
from jax.experimental import pallas as pl
from jax.experimental.pallas import tpu as pltpu
from jax.sharding import PartitionSpec as P

VMEM = pl.BlockSpec(memory_space=pltpu.VMEM)
HBM = pl.BlockSpec(memory_space=pltpu.HBM)
SMEM = pl.BlockSpec(memory_space=pltpu.SMEM)
MIB = 1024 * 1024
F32 = jnp.float32
BF16 = jnp.bfloat16


def exchange(array, axis, by):
    peers = lax.axis_size(axis)
    return lax.ppermute(array, axis, [(i, i ^ by) for i in range(peers)])


def hop(array, piece, stage):
    bins, srcs, cores = (lax.axis_size(a) for a in ("delay", "src", "tgt"))
    pairs = []
    for d in range(bins):
        for s in range(srcs):
            for t in range(cores):
                over_src = (piece + t + stage) % 2 == 0
                to = (d, s ^ 1) if over_src else (d ^ 1, s)
                pairs.append(
                    ((d * srcs + s) * cores + t, (to[0] * srcs + to[1]) * cores + t)
                )
    return lax.ppermute(array, ("delay", "src", "tgt"), pairs)


def call(kernel, outs, specs, scratch, *args, grant=32 * MIB):
    return list(pl.pallas_call(
        kernel,
        out_shape=outs,
        in_specs=specs,
        out_specs=[VMEM] * len(outs),
        scratch_shapes=scratch,
        compiler_params=pltpu.CompilerParams(vmem_limit_bytes=grant),
    )(*args))


class Plan:
    def __init__(self, blocks, history):
        self.edge = blocks.shape[-1]
        self.slots = blocks.shape[3]
        self.owned = history.shape[2]
        self.width = history.shape[3]
        self.srcs = lax.axis_size("src")
        self.bins = lax.axis_size("delay")
        self.halves = history.shape[1]
        owned_blocks = self.owned // self.edge
        self.groups = min(self.bins // 2, owned_blocks // 2)
        self.slice_rows = self.owned // (2 * self.groups)
        self.piece = self.slice_rows // 2
        self.tile_rows = self.owned * self.srcs
        self.slices = 2 * self.groups

    def x(self):
        return lax.axis_index("delay") & 1

    def g(self):
        return (lax.axis_index("delay") >> 1) & (self.groups - 1)

    def shape(self, *lead):
        return jax.ShapeDtypeStruct((*lead, self.piece, self.width), BF16)


GROUP = 16


def tile_product(p, acc, blocks, coords, counts, column, ready=None):
    def group(i, carry):
        if ready is not None:
            ready(i)
        slots = [i * GROUP + j for j in range(GROUP)]
        products = [
            jnp.dot(blocks[c], column(coords[1, c]), preferred_element_type=F32)
            for c in slots
        ]
        for c, product in zip(slots, products):
            at = pl.ds(pl.multiple_of(coords[0, c] * p.edge, p.edge), p.edge)
            acc[at] += jnp.where(c < counts[0], product, 0.0)
        return carry

    lax.fori_loop(0, p.slots // GROUP, group, 0, unroll=ready is None)


def over_src(piece):
    return ((lax.axis_index("tgt") + piece) & 1) == 0


def split_first(p, source, outs, high):
    y, x = lax.axis_index("src") & 1, p.x()

    def rows(s, xx, g, piece):
        start = (((high * 2 + s) * 2 + xx) * p.groups + g) * p.slice_rows
        start = pl.multiple_of(start + piece * p.piece, p.piece)
        return source[pl.ds(start, p.piece)].astype(BF16)

    for piece in range(2):
        far, near, keep, stay = outs[4 * piece : 4 * piece + 4]
        by_src = over_src(piece)
        for g in range(p.groups):
            far[g] = rows(y ^ 1, x ^ 1, g, piece)
            near[g] = rows(jnp.where(by_src, y ^ 1, y), jnp.where(by_src, x, x ^ 1), g, piece)
            keep[g] = rows(jnp.where(by_src, y, y ^ 1), jnp.where(by_src, x ^ 1, x), g, piece)
            stay[g] = rows(y, x, g, piece)


def split_kernel(p, source, *outs):
    split_first(p, source, outs, 0)


def hand_over(p, acc, outs):
    if p.srcs == 2:
        split_first(p, acc, outs, 0)
    else:
        outs[0][...] = acc[...].astype(BF16)


def first_kernel(p, blocks_hbm, coords_hbm, counts, history_hbm, *rest):
    *outs, own_half, acc, blocks, history, coords, block_sem, history_sem, coords_sem = rest
    per_half = p.owned // p.edge
    rows = p.owned // 2
    copies = [
        pltpu.make_async_copy(
            history_hbm.at[h, pl.ds(i * rows, rows)],
            history.at[h, pl.ds(i * rows, rows)],
            history_sem.at[h, i],
        )
        for h in range(p.halves)
        for i in range(2)
    ]

    def block_copy(i):
        at = pl.ds(i * GROUP, GROUP)
        return pltpu.make_async_copy(blocks_hbm.at[at], blocks.at[at], block_sem.at[i])

    copies.append(pltpu.make_async_copy(coords_hbm, coords, coords_sem))
    for copy in copies:
        copy.start()
    for i in range(p.slots // GROUP):
        block_copy(i).start()
    acc[...] = jnp.zeros_like(acc)
    for copy in copies:
        copy.wait()

    def column(c):
        start = pl.multiple_of((c % per_half) * p.edge, p.edge)
        return history[c // per_half, pl.ds(start, p.edge)]

    tile_product(p, acc, blocks, coords, counts, column, lambda i: block_copy(i).wait())
    own_half[...] = history[lax.axis_index("tgt")]
    hand_over(p, acc, outs)


def later_kernel(p, blocks, coords, counts, own, other, *rest):
    *outs, acc = rest
    per_half = p.owned // p.edge
    half = lax.axis_index("tgt")

    def column(c):
        start = pl.multiple_of((c % per_half) * p.edge, p.edge)
        at = pl.ds(start, p.edge)
        return jnp.where(c // per_half == half, own[at], other[at])

    acc[...] = jnp.zeros_like(acc)
    tile_product(p, acc, blocks, coords, counts, column)
    hand_over(p, acc, outs)


def total(*terms):
    value = terms[0].astype(F32)
    for term in terms[1:]:
        value = value + term.astype(F32)
    return value.astype(BF16)


def second_kernel(p, keep, came, send):
    send[...] = total(keep[...], came[...])


def third_kernel(p, *refs):
    ins, outs = refs[:6], refs[6:]
    if len(outs) > p.groups:
        mine, behind, *outs, onward = outs

        @pl.when(p.x() == 0)
        def _():
            onward[...] = mine[...]

        @pl.when(p.x() == 1)
        def _():
            onward[...] = behind[...]

    here = p.g()
    for k, ref in enumerate(outs):
        g = here ^ k
        for piece in range(2):
            ref[piece] = total(*(term[g] for term in ins[3 * piece : 3 * piece + 3]))


def current_kernel(p, step, keep, *refs):
    *came, excitation, inverse, out = refs
    start = (p.x() * p.groups + p.g()) * p.slice_rows
    per_slice = p.slice_rows // p.edge
    field = keep[...].astype(F32)
    for ref in came:
        field = field + ref[...].astype(F32)
    field = field.reshape(p.slice_rows, p.width)
    at = pl.ds(pl.multiple_of(start, p.slice_rows), p.slice_rows)
    drive = (excitation[step, 0, at].astype(F32) - field).astype(BF16)
    first = (p.x() * p.groups + p.g()) * per_slice
    for b in range(per_slice):
        rows = slice(b * p.edge, (b + 1) * p.edge)
        out[rows] = jnp.dot(
            inverse[0, first + b], drive[rows], preferred_element_type=F32
        ).astype(BF16)


def place_of(p, k):
    low = (lax.axis_index("delay") & (p.slices - 1)) ^ k
    at = ((low & 1) * p.groups + (low >> 1)) * p.slice_rows
    return pl.ds(pl.multiple_of(at, p.slice_rows), p.slice_rows)


def join_slices(p, slices, out):
    k = 0
    for ref in slices:
        for i in range(ref.shape[0] // p.slice_rows):
            by = 2 * (k % p.groups) + k // p.groups
            out[place_of(p, by)] = ref[i * p.slice_rows : (i + 1) * p.slice_rows]
            k += 1


def join_kernel(p, *refs):
    *slices, shifted, out, lagged = refs
    join_slices(p, slices, out)
    first_bin = lax.axis_index("delay") == 0

    @pl.when(first_bin)
    def _():
        lagged[...] = out[...]

    @pl.when(jnp.logical_not(first_bin))
    def _():
        lagged[...] = shifted[...]


def last_kernel(p, before, *refs):
    *slices, out = refs
    out[: before.shape[0], 0] = before[...]
    join_slices(p, slices, out.at[before.shape[0], 0])


def narrow(p, firsts):
    if p.srcs == 2:
        return firsts
    rest = firsts[0]
    by = p.srcs // 2
    while by > 1:
        upper = (lax.axis_index("src") // by) & 1
        size = rest.shape[0] // 2
        keep = lax.dynamic_slice_in_dim(rest, upper * size, size)
        send = lax.dynamic_slice_in_dim(rest, (1 - upper) * size, size)
        rest = total(keep, exchange(send, "src", by))
        by //= 2
    return call(
        functools.partial(split_kernel, p), [p.shape(p.groups)] * 8, [VMEM], [], rest
    )


def field_sum(p, firsts, lagged):
    moved = []
    if lagged is not None:
        behind = lax.ppermute(
            lagged, "delay", [(i, i + 2) for i in range(1, p.bins - 2, 2)]
        )
        moved = [lagged, behind]
    far0, near0, keep0, stay0, far1, near1, keep1, stay1 = narrow(p, firsts)
    far0, far1 = hop(far0, 0, 0), hop(far1, 1, 0)
    near0, near1 = hop(near0, 0, 0), hop(near1, 1, 0)
    one = [p.shape(p.groups)]
    second = functools.partial(second_kernel, p)
    (send0,) = call(second, one, [VMEM] * 2, [], keep0, far0)
    (send1,) = call(second, one, [VMEM] * 2, [], keep1, far1)
    terms = call(
        functools.partial(third_kernel, p),
        [p.shape(2)] * p.groups
        + [jax.ShapeDtypeStruct(v.shape, BF16) for v in moved[:1]],
        [VMEM] * (6 + len(moved)),
        [],
        stay0,
        near0,
        hop(send0, 0, 1),
        stay1,
        near1,
        hop(send1, 1, 1),
        *moved,
    )
    shifted = None
    if moved:
        shifted = exchange(terms.pop(), "delay", 1)
    by = 2 * p.groups
    while by < p.bins:
        terms = [
            (v.astype(F32) + exchange(v, "delay", by).astype(F32)).astype(BF16)
            for v in terms
        ]
        by *= 2
    keep, *sends = terms
    came = [exchange(v, "delay", 2 * k) for k, v in enumerate(sends, 1)]
    return [keep, *came], shifted


def pack_kernel(*refs):
    *ins, out = refs
    rows = ins[0].shape[0]
    for i, ref in enumerate(ins):
        out[i * rows : (i + 1) * rows] = ref[...]


def pack(p, parts):
    return call(
        pack_kernel,
        [jax.ShapeDtypeStruct((len(parts) * p.slice_rows, p.width), BF16)],
        [VMEM] * len(parts),
        [],
        *parts,
    )[0]


def gather(p, piece):
    along = [exchange(piece, "delay", 2 * k) for k in range(1, p.groups)]
    beside = exchange(piece, "delay", 1)
    over = [exchange(piece, "delay", 2 * k + 1) if k in (1,) else exchange(v, "delay", 1) for k, v in enumerate(along, 1)]
    return [piece, *along, beside, *over]


def shards(blocks, coords, counts, history, excitation, inverse):
    p = Plan(blocks, history)
    steps = excitation.shape[0]
    slot_blocks = blocks.reshape(blocks.shape[3:])
    places = coords.reshape(-1, 2).T
    used = counts.reshape(-1)
    first_outs = [p.shape(p.groups)] * 8
    if p.srcs > 2:
        first_outs = [jax.ShapeDtypeStruct((p.tile_rows, p.width), BF16)]
    half = jax.ShapeDtypeStruct((p.owned, p.width), BF16)
    acc = [pltpu.VMEM((p.tile_rows, p.width), F32)]
    *firsts, lagged = call(
        functools.partial(first_kernel, p),
        first_outs + [half],
        [HBM, HBM, SMEM, HBM],
        acc
        + [
            pltpu.VMEM(slot_blocks.shape, BF16),
            pltpu.VMEM(history.shape[1:], BF16),
            pltpu.SMEM(places.shape, places.dtype),
            pltpu.SemaphoreType.DMA((p.slots // GROUP,)),
            pltpu.SemaphoreType.DMA((p.halves, 2)),
            pltpu.SemaphoreType.DMA,
        ],
        slot_blocks,
        places,
        used,
        history[0],
        grant=52 * MIB,
    )
    done = []
    for step in range(steps):
        more = step + 1 < steps
        terms, shifted = field_sum(p, firsts, lagged if more else None)
        piece = call(
            functools.partial(current_kernel, p, step),
            [jax.ShapeDtypeStruct((p.slice_rows, p.width), BF16)],
            [VMEM] * (len(terms) + 2),
            [],
            *terms,
            excitation,
            inverse,
        )[0]
        slices = gather(p, piece)
        if not more:
            return call(
                functools.partial(last_kernel, p),
                [jax.ShapeDtypeStruct((steps, 1, p.owned, p.width), BF16)],
                [VMEM] * (1 + len(slices)),
                [],
                jnp.stack(done),
                *slices,
            )[0]
        current, lagged = call(
            functools.partial(join_kernel, p),
            [half, half],
            [VMEM] * (len(slices) + 1),
            [],
            *slices,
            shifted,
        )
        done.append(current)
        other = exchange(lagged, "tgt", 1)
        firsts = call(
            functools.partial(later_kernel, p),
            first_outs,
            [VMEM, SMEM, SMEM, VMEM, VMEM],
            acc,
            slot_blocks,
            places,
            used,
            lagged,
            other,
        )


def solution(mesh):
    placed = (
        P("delay", "src", "tgt", None, None, None),
        P("delay", "src", "tgt", None, None),
        P("delay", "src", "tgt"),
        P("delay", None, "src", None),
        P(None, "tgt", "src", None),
        P("tgt", "src", None, None),
    )
    return jax.shard_map(
        shards, mesh=mesh, in_specs=placed, out_specs=P(None, "tgt", "src", None), check_vma=False
    )
```

```python
import functools

import jax
import jax.numpy as jnp
from jax import lax
from jax.experimental import pallas as pl
from jax.experimental.pallas import tpu as pltpu
from jax.sharding import PartitionSpec as P

VMEM = pl.BlockSpec(memory_space=pltpu.VMEM)
HBM = pl.BlockSpec(memory_space=pltpu.HBM)
SMEM = pl.BlockSpec(memory_space=pltpu.SMEM)
MIB = 1024 * 1024
F32 = jnp.float32
BF16 = jnp.bfloat16


def exchange(array, axis, by):
    peers = lax.axis_size(axis)
    return lax.ppermute(array, axis, [(i, i ^ by) for i in range(peers)])


def hop(array, piece, stage):
    bins, srcs, cores = (lax.axis_size(a) for a in ("delay", "src", "tgt"))
    pairs = []
    for d in range(bins):
        for s in range(srcs):
            for t in range(cores):
                over_src = (piece + t + stage) % 2 == 0
                to = (d, s ^ 1) if over_src else (d ^ 1, s)
                pairs.append(
                    ((d * srcs + s) * cores + t, (to[0] * srcs + to[1]) * cores + t)
                )
    return lax.ppermute(array, ("delay", "src", "tgt"), pairs)


def along_g(p, array, k):
    cores = lax.axis_size("tgt")
    return lax.ppermute(
        array,
        ("delay", "tgt"),
        [
            (d * cores + t, (d ^ (2 * (k if t % 2 == 0 else p.groups - k))) * cores + t)
            for d in range(p.bins)
            for t in range(cores)
        ],
    )


def own_turn(p, k):
    return jnp.where(lax.axis_index("tgt") & 1 == 0, k, p.groups - k) if k else 0


def call(kernel, outs, specs, scratch, *args, grant=32 * MIB):
    return list(pl.pallas_call(
        kernel,
        out_shape=outs,
        in_specs=specs,
        out_specs=[VMEM] * len(outs),
        scratch_shapes=scratch,
        compiler_params=pltpu.CompilerParams(vmem_limit_bytes=grant),
    )(*args))


class Plan:
    def __init__(self, blocks, history):
        self.edge = blocks.shape[-1]
        self.slots = blocks.shape[3]
        self.owned = history.shape[2]
        self.width = history.shape[3]
        self.srcs = lax.axis_size("src")
        self.bins = lax.axis_size("delay")
        self.halves = history.shape[1]
        owned_blocks = self.owned // self.edge
        self.groups = min(self.bins // 2, owned_blocks // 2)
        self.slice_rows = self.owned // (2 * self.groups)
        self.piece = self.slice_rows // 2
        self.tile_rows = self.owned * self.srcs
        self.slices = 2 * self.groups

    def x(self):
        return lax.axis_index("delay") & 1

    def g(self):
        return (lax.axis_index("delay") >> 1) & (self.groups - 1)

    def shape(self, *lead):
        return jax.ShapeDtypeStruct((*lead, self.piece, self.width), BF16)


GROUP = 16


def tile_product(p, acc, blocks, coords, counts, column, ready=None):
    def group(i, carry):
        if ready is not None:
            ready(i)
        slots = [i * GROUP + j for j in range(GROUP)]
        products = [
            jnp.dot(blocks[c], column(coords[1, c]), preferred_element_type=F32)
            for c in slots
        ]
        for c, product in zip(slots, products):
            at = pl.ds(pl.multiple_of(coords[0, c] * p.edge, p.edge), p.edge)
            acc[at] += jnp.where(c < counts[0], product, 0.0)
        return carry

    lax.fori_loop(0, p.slots // GROUP, group, 0, unroll=ready is None)


def over_src(piece):
    return ((lax.axis_index("tgt") + piece) & 1) == 0


def split_first(p, source, outs, high):
    y, x = lax.axis_index("src") & 1, p.x()

    def rows(s, xx, g, piece):
        start = (((high * 2 + s) * 2 + xx) * p.groups + g) * p.slice_rows
        start = pl.multiple_of(start + piece * p.piece, p.piece)
        return source[pl.ds(start, p.piece)].astype(BF16)

    for piece in range(2):
        far, near, keep, stay = outs[4 * piece : 4 * piece + 4]
        by_src = over_src(piece)
        for g in range(p.groups):
            far[g] = rows(y ^ 1, x ^ 1, g, piece)
            near[g] = rows(jnp.where(by_src, y ^ 1, y), jnp.where(by_src, x, x ^ 1), g, piece)
            keep[g] = rows(jnp.where(by_src, y, y ^ 1), jnp.where(by_src, x ^ 1, x), g, piece)
            stay[g] = rows(y, x, g, piece)


def split_kernel(p, source, *outs):
    split_first(p, source, outs, 0)


def hand_over(p, acc, outs):
    if p.srcs == 2:
        split_first(p, acc, outs, 0)
    else:
        outs[0][...] = acc[...].astype(BF16)


def first_kernel(p, blocks_hbm, coords_hbm, counts, history_hbm, *rest):
    *outs, own_half, acc, blocks, history, coords, block_sem, history_sem, coords_sem = rest
    per_half = p.owned // p.edge
    rows = p.owned // 2
    copies = [
        pltpu.make_async_copy(
            history_hbm.at[h, pl.ds(i * rows, rows)],
            history.at[h, pl.ds(i * rows, rows)],
            history_sem.at[h, i],
        )
        for h in range(p.halves)
        for i in range(2)
    ]

    def block_copy(i):
        at = pl.ds(i * GROUP, GROUP)
        return pltpu.make_async_copy(blocks_hbm.at[at], blocks.at[at], block_sem.at[i])

    copies.append(pltpu.make_async_copy(coords_hbm, coords, coords_sem))
    for copy in copies:
        copy.start()
    for i in range(p.slots // GROUP):
        block_copy(i).start()
    acc[...] = jnp.zeros_like(acc)
    for copy in copies:
        copy.wait()

    def column(c):
        start = pl.multiple_of((c % per_half) * p.edge, p.edge)
        return history[c // per_half, pl.ds(start, p.edge)]

    tile_product(p, acc, blocks, coords, counts, column, lambda i: block_copy(i).wait())
    own_half[...] = history[lax.axis_index("tgt")]
    hand_over(p, acc, outs)


def later_kernel(p, blocks, coords, counts, own, other, *rest):
    *outs, acc = rest
    per_half = p.owned // p.edge
    half = lax.axis_index("tgt")

    def column(c):
        start = pl.multiple_of((c % per_half) * p.edge, p.edge)
        at = pl.ds(start, p.edge)
        return jnp.where(c // per_half == half, own[at], other[at])

    acc[...] = jnp.zeros_like(acc)
    tile_product(p, acc, blocks, coords, counts, column)
    hand_over(p, acc, outs)


def total(*terms):
    value = terms[0].astype(F32)
    for term in terms[1:]:
        value = value + term.astype(F32)
    return value.astype(BF16)


def second_kernel(p, keep, came, send):
    send[...] = total(keep[...], came[...])


def third_kernel(p, *refs):
    ins, outs = refs[:6], refs[6:]
    if len(outs) > p.groups:
        mine, behind, *outs, onward = outs

        @pl.when(p.x() == 0)
        def _():
            onward[...] = mine[...]

        @pl.when(p.x() == 1)
        def _():
            onward[...] = behind[...]

    here = p.g()
    for k, ref in enumerate(outs):
        g = here ^ own_turn(p, k)
        for piece in range(2):
            ref[piece] = total(*(term[g] for term in ins[3 * piece : 3 * piece + 3]))


def current_kernel(p, step, keep, *refs):
    *came, excitation, inverse, out = refs
    start = (p.x() * p.groups + p.g()) * p.slice_rows
    per_slice = p.slice_rows // p.edge
    field = keep[...].astype(F32)
    for ref in came:
        field = field + ref[...].astype(F32)
    field = field.reshape(p.slice_rows, p.width)
    at = pl.ds(pl.multiple_of(start, p.slice_rows), p.slice_rows)
    drive = (excitation[step, 0, at].astype(F32) - field).astype(BF16)
    first = (p.x() * p.groups + p.g()) * per_slice
    for b in range(per_slice):
        rows = slice(b * p.edge, (b + 1) * p.edge)
        out[rows] = jnp.dot(
            inverse[0, first + b], drive[rows], preferred_element_type=F32
        ).astype(BF16)


def place_of(p, k):
    low = (lax.axis_index("delay") & (p.slices - 1)) ^ k
    at = ((low & 1) * p.groups + (low >> 1)) * p.slice_rows
    return pl.ds(pl.multiple_of(at, p.slice_rows), p.slice_rows)


def join_slices(p, slices, out):
    k = 0
    for ref in slices:
        for i in range(ref.shape[0] // p.slice_rows):
            by = 2 * (k % p.groups) + k // p.groups
            out[place_of(p, by)] = ref[i * p.slice_rows : (i + 1) * p.slice_rows]
            k += 1


def join_kernel(p, *refs):
    *slices, shifted, out, lagged = refs
    join_slices(p, slices, out)
    first_bin = lax.axis_index("delay") == 0

    @pl.when(first_bin)
    def _():
        lagged[...] = out[...]

    @pl.when(jnp.logical_not(first_bin))
    def _():
        lagged[...] = shifted[...]


def last_kernel(p, before, *refs):
    *slices, out = refs
    out[: before.shape[0], 0] = before[...]
    join_slices(p, slices, out.at[before.shape[0], 0])


def narrow(p, firsts):
    if p.srcs == 2:
        return firsts
    rest = firsts[0]
    by = p.srcs // 2
    while by > 1:
        upper = (lax.axis_index("src") // by) & 1
        size = rest.shape[0] // 2
        keep = lax.dynamic_slice_in_dim(rest, upper * size, size)
        send = lax.dynamic_slice_in_dim(rest, (1 - upper) * size, size)
        rest = total(keep, exchange(send, "src", by))
        by //= 2
    return call(
        functools.partial(split_kernel, p), [p.shape(p.groups)] * 8, [VMEM], [], rest
    )


def field_sum(p, firsts, lagged):
    moved = []
    if lagged is not None:
        behind = lax.ppermute(
            lagged, "delay", [(i, i + 2) for i in range(1, p.bins - 2, 2)]
        )
        moved = [lagged, behind]
    far0, near0, keep0, stay0, far1, near1, keep1, stay1 = narrow(p, firsts)
    far0, far1 = hop(far0, 0, 0), hop(far1, 1, 0)
    near0, near1 = hop(near0, 0, 0), hop(near1, 1, 0)
    one = [p.shape(p.groups)]
    second = functools.partial(second_kernel, p)
    (send0,) = call(second, one, [VMEM] * 2, [], keep0, far0)
    (send1,) = call(second, one, [VMEM] * 2, [], keep1, far1)
    terms = call(
        functools.partial(third_kernel, p),
        [p.shape(2)] * p.groups
        + [jax.ShapeDtypeStruct(v.shape, BF16) for v in moved[:1]],
        [VMEM] * (6 + len(moved)),
        [],
        stay0,
        near0,
        hop(send0, 0, 1),
        stay1,
        near1,
        hop(send1, 1, 1),
        *moved,
    )
    shifted = None
    if moved:
        shifted = exchange(terms.pop(), "delay", 1)
    by = 2 * p.groups
    while by < p.bins:
        terms = [
            (v.astype(F32) + exchange(v, "delay", by).astype(F32)).astype(BF16)
            for v in terms
        ]
        by *= 2
    keep, *sends = terms
    came = [along_g(p, v, k) for k, v in enumerate(sends, 1)]
    return [keep, *came], shifted


def pack_kernel(*refs):
    *ins, out = refs
    rows = ins[0].shape[0]
    for i, ref in enumerate(ins):
        out[i * rows : (i + 1) * rows] = ref[...]


def pack(p, parts):
    return call(
        pack_kernel,
        [jax.ShapeDtypeStruct((len(parts) * p.slice_rows, p.width), BF16)],
        [VMEM] * len(parts),
        [],
        *parts,
    )[0]


def gather(p, piece):
    along = [exchange(piece, "delay", 2 * k) for k in range(1, p.groups)]
    beside = exchange(piece, "delay", 1)
    over = [exchange(piece, "delay", 2 * k + 1) if k in (1,) else exchange(v, "delay", 1) for k, v in enumerate(along, 1)]
    return [piece, *along, beside, *over]


def shards(blocks, coords, counts, history, excitation, inverse):
    p = Plan(blocks, history)
    steps = excitation.shape[0]
    slot_blocks = blocks.reshape(blocks.shape[3:])
    places = coords.reshape(-1, 2).T
    used = counts.reshape(-1)
    first_outs = [p.shape(p.groups)] * 8
    if p.srcs > 2:
        first_outs = [jax.ShapeDtypeStruct((p.tile_rows, p.width), BF16)]
    half = jax.ShapeDtypeStruct((p.owned, p.width), BF16)
    acc = [pltpu.VMEM((p.tile_rows, p.width), F32)]
    *firsts, lagged = call(
        functools.partial(first_kernel, p),
        first_outs + [half],
        [HBM, HBM, SMEM, HBM],
        acc
        + [
            pltpu.VMEM(slot_blocks.shape, BF16),
            pltpu.VMEM(history.shape[1:], BF16),
            pltpu.SMEM(places.shape, places.dtype),
            pltpu.SemaphoreType.DMA((p.slots // GROUP,)),
            pltpu.SemaphoreType.DMA((p.halves, 2)),
            pltpu.SemaphoreType.DMA,
        ],
        slot_blocks,
        places,
        used,
        history[0],
        grant=52 * MIB,
    )
    done = []
    for step in range(steps):
        more = step + 1 < steps
        terms, shifted = field_sum(p, firsts, lagged if more else None)
        piece = call(
            functools.partial(current_kernel, p, step),
            [jax.ShapeDtypeStruct((p.slice_rows, p.width), BF16)],
            [VMEM] * (len(terms) + 2),
            [],
            *terms,
            excitation,
            inverse,
        )[0]
        slices = gather(p, piece)
        if not more:
            return call(
                functools.partial(last_kernel, p),
                [jax.ShapeDtypeStruct((steps, 1, p.owned, p.width), BF16)],
                [VMEM] * (1 + len(slices)),
                [],
                jnp.stack(done),
                *slices,
            )[0]
        current, lagged = call(
            functools.partial(join_kernel, p),
            [half, half],
            [VMEM] * (len(slices) + 1),
            [],
            *slices,
            shifted,
        )
        done.append(current)
        other = exchange(lagged, "tgt", 1)
        firsts = call(
            functools.partial(later_kernel, p),
            first_outs,
            [VMEM, SMEM, SMEM, VMEM, VMEM],
            acc,
            slot_blocks,
            places,
            used,
            lagged,
            other,
        )


def solution(mesh):
    placed = (
        P("delay", "src", "tgt", None, None, None),
        P("delay", "src", "tgt", None, None),
        P("delay", "src", "tgt"),
        P("delay", None, "src", None),
        P(None, "tgt", "src", None),
        P("tgt", "src", None, None),
    )
    return jax.shard_map(
        shards, mesh=mesh, in_specs=placed, out_specs=P(None, "tgt", "src", None), check_vma=False
    )
```
